32 devices in a mesh: seq: 8 (over y, x, core), exp: 4 (over z).
Axes of the slice: x: 2, y: 2, z: 4, core: 2. Of those that a mesh axis runs over, the one named last changes fastest.
Arguments:
- qk_proj: bfloat16 [1024, 2, 2048], P('seq', None, 'exp'), may hold values from -6 to 6
- v_proj: bfloat16 [1024, 4096], P('seq', 'exp'), may hold values from -6 to 6
- z_proj: bfloat16 [1024, 4096], P('seq', 'exp'), may hold values from -6 to 6
- conv_qk: float32 [4, 2, 2048], P(None, None, 'exp'), may hold values from -3 to 3
- conv_v: float32 [4, 4096], P(None, 'exp'), may hold values from -3 to 3
- decay_log: float32 [32, 1024], P('exp', 'seq'), may hold values from -2 to 0
- beta_gate: float32 [32, 1024], P('exp', 'seq'), may hold values from 0.05 to 0.95
- doc_ids: int32 [1024], replicated, may hold values from 0 to 7, never falling along the last dimension, each value on 1 to 256 neighbouring positions
- head_gain: float32 [128], replicated, may hold values from 0.1 to 1.9
- out_weight: bfloat16 [4096, 2048], P('exp'), may hold values from -0.09375 to 0.09375
- residual: bfloat16 [1024, 2048], P(('seq', 'exp')), may hold values from -6 to 6
- post_gain: float32 [2048], replicated, may hold values from 0.1 to 1.9
- route_ids: int32 [1024, 10], P(('seq', 'exp')), may hold values from 0 to 63, all different within a row; in each aligned block of 32 rows (0 to 31, 32 to 63, ...) at most 8 rows name the same one
- route_weight: float32 [1024, 10], P(('seq', 'exp')), may hold values from 0.02 to 0.3
- expert_gate_up: bfloat16 [64, 2, 2048, 512], P(('seq', 'exp')), may hold values from -0.125 to 0.125
- expert_down: bfloat16 [64, 512, 2048], P(('seq', 'exp')), may hold values from -0.25 to 0.25
- shared_gate_up: bfloat16 [2, 2048, 512], replicated, may hold values from -0.125 to 0.125
- shared_down: bfloat16 [512, 2048], replicated, may hold values from -0.25 to 0.25
- shared_gate: float32 [2048], replicated, may hold values from -0.125 to 0.125
Outputs:
- hidden_mid: bfloat16 [1024, 2048], P(('seq', 'exp'))
- moe_out: bfloat16 [1024, 2048], P(('seq', 'exp'))
The draws below stay inside these ranges and needn't reach their ends.
Inputs may be any that keep to these rules, and one draw needn't show every extreme that they name: `route_ids`: each row names 10 different experts. In each aligned block of 32 rows (the rows of one device) no expert is named by more than 8 rows, and in some blocks an expert is named by exactly 8 rows. `doc_ids`: document numbers never fall along the stream; each document covers 1 to 256 tokens, and one covers exactly 256.
All inputs are finite; a program needn't handle non-finite values.
Results may differ from the reference program's by a relative error of at most 0.0075.
Values may be sent and summed in bfloat16 or wider, within the bound.
A program may use at most 128 MiB of HBM per device.

```python
import math
import jax
import jax.numpy as jnp
import numpy as np
from jax import lax

D = 2048
VALUE_HEADS = 32
DV = 128
KCONV = 4
GROUP = 64
EFF = 512
EFF_SH = 512
TOPK = 10
TOK_DEV = 128
STREAM_TOKENS = 1024
KEYS = 2048
VALS = 4096
EXPERTS = 64
ROWS_DEV = 32
CAP = 8
DOCS = 8
DOC_MOST = 256
N_EXP = 4


def draw_decay_log(key, part):
    key_sequence = jax.random.split(key, 7)
    fast_share = 0.5
    chooser = jax.random.uniform(key_sequence[0], (VALUE_HEADS, 1))
    fast_rate = jnp.exp(jax.random.uniform(key_sequence[1], (VALUE_HEADS, 1), minval=math.log(math.log(10.0) / 50.0), maxval=math.log(math.log(10.0) / 30.0)))
    slow_total = jnp.exp(jax.random.uniform(key_sequence[2], (VALUE_HEADS, 1), minval=math.log(0.02), maxval=math.log(0.3)))
    slow_rate = slow_total / STREAM_TOKENS
    device_count = STREAM_TOKENS // TOK_DEV
    window_len = min(32, TOK_DEV // 2)
    window_start = jax.random.randint(key_sequence[6], (VALUE_HEADS, device_count), 0, TOK_DEV - window_len + 1)
    token_position = jnp.arange(STREAM_TOKENS)
    token_offset = token_position % TOK_DEV
    start_per_token = jnp.repeat(window_start, TOK_DEV, axis=1)
    inside_window = (token_offset[None, :] >= start_per_token) & (token_offset[None, :] < start_per_token + window_len)
    baseline_rate = jnp.where((chooser < fast_share) & inside_window, fast_rate, slow_rate)
    jaggedness = jnp.exp(jax.random.uniform(key_sequence[3], (VALUE_HEADS, STREAM_TOKENS), minval=math.log(0.5), maxval=math.log(2.0)))
    spike_position = jax.random.randint(key_sequence[4], (VALUE_HEADS, 2), 0, STREAM_TOKENS)
    spike_length = jax.random.uniform(key_sequence[5], (VALUE_HEADS, 2), minval=0.22, maxval=0.69)
    spike_penalty = jnp.sum(jnp.where(token_position[None, :, None] == spike_position[:, None, :], spike_length[:, None, :], 0.0), axis=2)
    return (-(baseline_rate * jaggedness + spike_penalty)).astype(jnp.float32)


def levels(key, extent, shards, low, top_value):
    def one(position, blocks):
        draws = jax.random.uniform(jax.random.fold_in(jax.random.fold_in(key, 6), position), (blocks,), jnp.float32, low / len(shards), top_value / len(shards))
        return jnp.repeat(jnp.exp(draws), extent[position] // blocks).reshape((-1,) + (1,) * (len(extent) - position - 1))

    factor_of = one(*shards[0])
    for cut in shards[1:]:
        factor_of = factor_of * one(*cut)
    return factor_of


def length_profile(amount, total, limit, lean):
    loads = [(1 << 20) // math.isqrt(rank ** lean) + 1 for rank in range(2, amount + 1)]
    spare, given = total - limit - (amount - 1), [1] * (amount - 1)
    while spare > 0:
        free = [i for i in range(amount - 1) if given[i] < limit]
        mass, left = sum([loads[i] for i in free]), spare
        for i in free:
            more = min(limit - given[i], max(1, left * loads[i] // mass), spare)
            given[i] = given[i] + more
            spare = spare - more
    return np.array([limit] + given)


def ragged_sizes(key, amount, total, bound, slope):
    if amount == 2:
        one = jax.random.randint(key, (), max(1, total - bound), min(bound, total - 1) + 1)
        return jnp.stack([one, total - one])
    sizes = jnp.asarray(length_profile(amount, total, bound, slope), jnp.int32)
    couples = (amount - 1) // 2
    donor, taker = sizes[1:1 + 2 * couples:2], sizes[2:2 + 2 * couples:2]
    slack = jnp.minimum(donor - 1, bound - taker)
    passed = jax.random.randint(jax.random.fold_in(key, 1), (couples,), 0, 1 << 20) % (slack + 1)
    sizes = sizes.at[1:1 + 2 * couples:2].set(donor - passed).at[2:2 + 2 * couples:2].set(taker + passed)
    return sizes[jax.random.permutation(jax.random.fold_in(key, 2), amount)]


def routed_block(own_key, own, number, rows, count, top, most, lean):
    order = jax.random.permutation(own_key, count)
    packed, usual = load_shares(count, rows * top, most, lean, True), load_shares(count, rows * top, most, lean, False)
    places = jnp.arange(count)

    def named(tallies, rotation):
        used = int((tallies > 0).sum())
        fixed = max(1, used // 4)
        passed = fixed + (places - fixed + rotation * (used - fixed)) % max(1, count - fixed)
        return jnp.zeros((count,), jnp.int32).at[order[jnp.where(places < fixed, places, passed)]].set(jnp.asarray(tallies, jnp.int32))

    tallies = jnp.where(number % 4 == 0, named(packed, number // 4), named(usual, number - number // 4 - 1))
    mixed = jax.random.permutation(jax.random.fold_in(own, 3), count)
    donor, sink = mixed[0:count // 2 * 2:2], mixed[1:count // 2 * 2:2]
    margin = jnp.minimum(tallies[donor] - 1, most - tallies[sink]) // 2
    margin = jnp.where((donor == order[0]) | (sink == order[0]) | (tallies[sink] == 0), 0, jnp.maximum(margin, 0))
    passed = jax.random.randint(jax.random.fold_in(own, 4), (count // 2,), 0, 1 << 20) % (margin + 1)
    tallies = tallies.at[donor].add(-passed).at[sink].add(passed)
    labels = jnp.searchsorted(jnp.cumsum(tallies), jnp.arange(rows * top), side="right").astype(jnp.int32)
    table = labels.reshape(top, rows).T
    table = table[jax.random.permutation(jax.random.fold_in(own, 1), rows)]
    rotation = jax.random.randint(jax.random.fold_in(own, 2), (rows, 1), 0, top)
    return jnp.take_along_axis(table, (jnp.arange(top)[None, :] + rotation) % top, axis=1)


def load_shares(amount, total, limit, lean, full):
    weights = [(1 << 20) // math.isqrt(standing ** lean) + 1 for standing in range(1, amount + 1)]
    largest = limit if full else min(limit, max(-(-total // amount), total * weights[0] // sum(weights)))
    least = 1 if total - largest >= amount - 1 else 0
    holding, rest = [largest] + [least] * (amount - 1), total - largest - least * (amount - 1)
    while rest > 0:
        free = [i for i in range(1, amount) if holding[i] < largest] or [i for i in range(1, amount) if holding[i] < limit]
        pool, left = sum([weights[i] for i in free]), rest
        for i in free:
            extra = min(limit - holding[i], max(1, left * weights[i] // pool), rest)
            holding[i] = holding[i] + extra
            rest = rest - extra
    return np.array(holding)


def centred(stream_key, extent, width, limit, cuts=(), held_as=jnp.bfloat16):
    entries = jax.random.normal(stream_key, extent, jnp.float32) * width
    if len(cuts) > 0:
        entries = levels(stream_key, extent, cuts, -0.22, 0.18) * entries
    return jnp.clip(entries, min=-limit, max=limit).astype(held_as)


def setup_inputs(seed: int = 0) -> dict:
    key_list = jax.random.split(jax.random.key(seed), 20)
    qk_proj = centred(key_list[0], (STREAM_TOKENS, 2, KEYS), 1.0, 6.0, ((0, 8), (2, 4)))
    v_proj = centred(key_list[1], (STREAM_TOKENS, VALS), 1.0, 6.0, ((0, 8), (1, 4)))
    z_proj = centred(key_list[2], (STREAM_TOKENS, VALS), 1.0, 6.0, ((0, 8), (1, 4)))
    conv_qk = centred(key_list[3], (KCONV, 2, KEYS), KCONV ** -0.5, 3.0, ((2, 4),), jnp.float32)
    conv_v = centred(key_list[4], (KCONV, VALS), KCONV ** -0.5, 3.0, ((1, 4),), jnp.float32)
    decay_log = draw_decay_log(jax.random.fold_in(key_list[19], 71), 0)
    beta_gate = jnp.clip(0.05 + 0.9 * jax.random.uniform(key_list[6], (VALUE_HEADS, STREAM_TOKENS), jnp.float32) ** levels(key_list[6], (VALUE_HEADS, STREAM_TOKENS), ((0, 4), (1, 8)), -0.2, 0.2), 0.05, 0.95)
    doc_ids = jnp.searchsorted(jnp.cumsum(ragged_sizes(key_list[7], DOCS, STREAM_TOKENS, DOC_MOST, 1)), jnp.arange(STREAM_TOKENS), side="right").astype(jnp.int32)
    head_gain = jnp.clip(1.0 + 0.18 * jax.random.normal(key_list[8], (DV,), jnp.float32), 0.1, 1.9)
    out_weight = centred(key_list[9], (VALS, D), VALS ** -0.5, 0.09375, ((0, 4),))
    residual = centred(key_list[10], (STREAM_TOKENS, D), 1.0, 6.0, ((0, 32),))
    post_gain = jnp.clip(1.0 + 0.18 * jax.random.normal(key_list[11], (D,), jnp.float32), 0.1, 1.9)
    route_ids_keys = jax.random.split(jax.random.fold_in(key_list[12], 1), STREAM_TOKENS // ROWS_DEV)
    route_ids_turns = jax.random.permutation(jax.random.fold_in(key_list[12], 3), STREAM_TOKENS // ROWS_DEV)
    route_ids = jax.vmap(lambda own, number: routed_block(jax.random.fold_in(key_list[12], 2), own, number, ROWS_DEV, EXPERTS, TOPK, CAP, 2))(route_ids_keys, route_ids_turns).reshape((STREAM_TOKENS, TOPK))
    route_weight = jnp.clip(jnp.exp(math.log(0.3) - 2.7080503 * jax.random.uniform(key_list[13], (STREAM_TOKENS, TOPK), jnp.float32) ** levels(key_list[13], (STREAM_TOKENS, TOPK), ((0, 32),), -0.2, 0.2)), 0.02, 0.3)
    expert_gate_up = centred(key_list[14], (EXPERTS, 2, D, EFF), D ** -0.5, 0.125, ((0, 32),))
    expert_down = centred(key_list[15], (EXPERTS, EFF, D), EFF ** -0.5, 0.25, ((0, 32),))
    shared_gate_up = centred(key_list[16], (2, D, EFF_SH), D ** -0.5, 0.125)
    shared_down = centred(key_list[17], (EFF_SH, D), EFF_SH ** -0.5, 0.25)
    shared_gate = centred(key_list[18], (D,), D ** -0.5, 0.125, (), jnp.float32)
    return dict(qk_proj=qk_proj, v_proj=v_proj, z_proj=z_proj, conv_qk=conv_qk, conv_v=conv_v, decay_log=decay_log, beta_gate=beta_gate, doc_ids=doc_ids, head_gain=head_gain, out_weight=out_weight, residual=residual, post_gain=post_gain, route_ids=route_ids, route_weight=route_weight, expert_gate_up=expert_gate_up, expert_down=expert_down, shared_gate_up=shared_gate_up, shared_down=shared_down, shared_gate=shared_gate)


exact_result = lax.Precision.HIGHEST

def causal_conv(extended, weight, doc_window):
    kernel_len = weight.shape[0]
    length = extended.shape[0] - kernel_len + 1
    own_doc = doc_window[kernel_len - 1:]
    summed = jnp.zeros((length,) + extended.shape[1:], jnp.float32)
    for tap_index in range(kernel_len):
        same_doc = (doc_window[tap_index:tap_index + length] == own_doc).astype(jnp.float32)
        same_doc = same_doc.reshape((length,) + (1,) * (extended.ndim - 1))
        summed = summed + weight[tap_index] * (extended[tap_index:tap_index + length].astype(jnp.float32) * same_doc)
    return jax.nn.silu(summed)

def prepare(qk_conv, v_conv, decay_log, beta_gate, doc_window, block_len):
    length = v_conv.shape[0]
    head_count = decay_log.shape[0]
    key_heads = head_count // 2
    key_dim = qk_conv.shape[2] // key_heads
    value_dim = v_conv.shape[1] // head_count
    split_qk = qk_conv.reshape(length, 2, key_heads, key_dim)
    unit_qk = split_qk * lax.rsqrt(lax.optimization_barrier(jnp.sum(split_qk * split_qk, axis=-1, keepdims=True)) + 1e-06)
    blocks = length // block_len

    def heads_first(tensor):
        return jnp.transpose(tensor, (1, 0, 2)).reshape(head_count, blocks, block_len, tensor.shape[2])
    queries = heads_first(jnp.repeat(unit_qk[:, 0], 2, axis=1) * key_dim ** (-0.5))
    key_vecs = heads_first(jnp.repeat(unit_qk[:, 1], 2, axis=1))
    values = heads_first(v_conv.reshape(length, head_count, value_dim))
    decays = decay_log.reshape(head_count, blocks, block_len)
    rates = beta_gate.reshape(head_count, blocks, block_len)
    kernel_len = doc_window.shape[0] - length + 1
    seg_block = doc_window[kernel_len - 1:].reshape(blocks, block_len)
    seg_before = doc_window[kernel_len - 2:kernel_len - 2 + length:block_len]
    return (queries, key_vecs, values, decays, rates, seg_block, seg_before)

def delta_blocks(queries, key_vecs, values, decays, rates, seg_block, seg_before):
    block_len = key_vecs.shape[2]
    value_dim = values.shape[3]
    cum_decay = jnp.cumsum(decays, axis=-1)
    lower_incl = jnp.tril(jnp.ones((block_len, block_len), dtype=bool))
    strict_lower = jnp.tril(jnp.ones((block_len, block_len), dtype=bool), -1)
    same_doc = seg_block[:, :, None] == seg_block[:, None, :]
    keep_mask = same_doc & lower_incl
    spread = cum_decay[..., :, None] - cum_decay[..., None, :]
    within = jnp.exp(jnp.where(keep_mask, spread, 0.0)) * keep_mask
    carried = jnp.exp(cum_decay) * (seg_block == seg_before[:, None])
    key_dots = jnp.einsum('hnik,hnjk->hnij', key_vecs, key_vecs, precision=exact_result)
    system = jnp.eye(block_len, dtype=jnp.float32) + rates[..., :, None] * within * key_dots * strict_lower
    right_sides = jnp.concatenate([rates[..., None] * values, (rates * carried)[..., None] * key_vecs], axis=-1)
    solved = jax.scipy.linalg.solve_triangular(system, right_sides, lower=True, unit_diagonal=True)
    new_values = solved[..., :value_dim]
    key_weights = solved[..., value_dim:]
    scores = jnp.einsum('hnik,hnjk->hnij', queries, key_vecs, precision=exact_result) * within
    out_local = jnp.einsum('hnij,hnjv->hniv', scores, new_values, precision=exact_result)
    query_eff = carried[..., None] * queries - jnp.einsum('hnij,hnjk->hnik', scores, key_weights, precision=exact_result)
    end_keys = within[..., -1, :][..., None] * key_vecs
    transit = carried[..., -1][..., None, None] * jnp.eye(key_vecs.shape[3], dtype=jnp.float32) - jnp.einsum('hnjk,hnjl->hnkl', end_keys, key_weights, precision=exact_result)
    offset = jnp.einsum('hnjk,hnjv->hnkv', end_keys, new_values, precision=exact_result)
    return (out_local, query_eff, transit, offset)

def run_blocks(query_eff, out_local, transit, offset, start_state):

    def advance(current_state, pieces):
        effective_query, local_output, permute_matrix, beta_matrix = pieces
        layer_output = jnp.einsum('mjw,mwq->mjq', effective_query, current_state, precision=exact_result) + local_output
        following_state = jnp.einsum('jyu,jug->jyg', permute_matrix, current_state, precision=exact_result) + beta_matrix
        return (following_state, layer_output)
    stacked = (jnp.moveaxis(query_eff, 1, 0), jnp.moveaxis(out_local, 1, 0), jnp.moveaxis(transit, 1, 0), jnp.moveaxis(offset, 1, 0))
    last_state, outputs = lax.scan(advance, start_state, stacked)
    return outputs

def gated_norm(outputs, z_proj, head_gain):
    blocks, head_count, block_len, value_dim = outputs.shape
    attn_heads = jnp.transpose(outputs, (0, 2, 1, 3)).reshape(blocks * block_len, head_count, value_dim)
    gate_z = z_proj.reshape(blocks * block_len, head_count, value_dim).astype(jnp.float32)
    scaled = attn_heads * lax.rsqrt(lax.optimization_barrier(jnp.mean(attn_heads * attn_heads, axis=-1, keepdims=True)) + 1e-06) * head_gain * jax.nn.silu(gate_z)
    return scaled.reshape(blocks * block_len, head_count * value_dim).astype(jnp.bfloat16)

def rms_scale(hidden, gain):
    return (hidden * lax.rsqrt(lax.optimization_barrier(jnp.mean(hidden * hidden, axis=-1, keepdims=True)) + 1e-06) * gain).astype(jnp.bfloat16)

def reference(qk_proj, v_proj, z_proj, conv_qk, conv_v, decay_log, beta_gate, doc_ids, head_gain, out_weight, residual, post_gain, route_ids, route_weight, expert_gate_up, expert_down, shared_gate_up, shared_down, shared_gate):
    kernel_len = conv_qk.shape[0]
    doc_window = jnp.concatenate([jnp.full((kernel_len - 1,), -1, jnp.int32), doc_ids.astype(jnp.int32)])
    qk_ext = jnp.concatenate([jnp.zeros((kernel_len - 1,) + qk_proj.shape[1:], qk_proj.dtype), qk_proj], axis=0)
    v_ext = jnp.concatenate([jnp.zeros((kernel_len - 1,) + v_proj.shape[1:], v_proj.dtype), v_proj], axis=0)
    qk_conv = causal_conv(qk_ext, conv_qk, doc_window)
    v_conv = causal_conv(v_ext, conv_v, doc_window)
    queries, key_vecs, values, decays, rates, seg_block, seg_before = prepare(qk_conv, v_conv, decay_log, beta_gate, doc_window, GROUP)
    out_local, query_eff, transit, offset = delta_blocks(queries, key_vecs, values, decays, rates, seg_block, seg_before)
    start_state = jnp.zeros((transit.shape[0], transit.shape[2], offset.shape[3]), jnp.float32)
    outputs = run_blocks(query_eff, out_local, transit, offset, start_state)
    gated = gated_norm(outputs, z_proj, head_gain)
    hidden = residual.astype(jnp.float32) + jnp.dot(gated.astype(jnp.float32), out_weight.astype(jnp.float32), preferred_element_type=jnp.float32)
    normed = rms_scale(hidden, post_gain)
    model_width = normed.shape[1]
    block_rows = TOK_DEV // N_EXP
    block_count = STREAM_TOKENS // block_rows
    pair_count = block_rows * TOPK
    pair_index = jnp.arange(pair_count, dtype=jnp.int32)

    def block_rank(block_ids):
        earlier = (block_ids[:, None] == block_ids[None, :]) & (pair_index[None, :] < pair_index[:, None])
        return lax.optimization_barrier(jnp.sum(earlier.astype(jnp.int32), axis=1))
    slot_rank = lax.map(block_rank, route_ids.reshape(block_count, pair_count)).reshape(-1)
    flat_ids = route_ids.reshape(-1)
    all_pairs = jnp.arange(STREAM_TOKENS * TOPK, dtype=jnp.int32)
    column = all_pairs // pair_count * CAP + slot_rank
    slot_table = jnp.full((EXPERTS, block_count * CAP), STREAM_TOKENS, jnp.int32).at[flat_ids, column].set(all_pairs // TOPK)
    padded_in = jnp.concatenate([normed, jnp.zeros((1, model_width), normed.dtype)], axis=0)

    def one_expert(pieces):
        slot_rows, gate_up, down_rows = pieces
        rows_in = padded_in[slot_rows]
        gate_half = jnp.dot(rows_in.astype(jnp.float32), gate_up[0].astype(jnp.float32), preferred_element_type=jnp.float32)
        up_half = jnp.dot(rows_in.astype(jnp.float32), gate_up[1].astype(jnp.float32), preferred_element_type=jnp.float32)
        activated = (jax.nn.silu(gate_half) * up_half).astype(jnp.bfloat16)
        return jnp.dot(activated.astype(jnp.float32), down_rows.astype(jnp.float32), preferred_element_type=jnp.float32).astype(jnp.bfloat16)
    expert_out = lax.map(one_expert, (slot_table, expert_gate_up, expert_down))
    picked = expert_out[flat_ids, column].reshape(STREAM_TOKENS, TOPK, model_width)
    weighted = lax.optimization_barrier(jnp.sum(route_weight[..., None] * picked.astype(jnp.float32), axis=1))
    shared_gate_half = jnp.dot(normed.astype(jnp.float32), shared_gate_up[0].astype(jnp.float32), preferred_element_type=jnp.float32)
    shared_up_half = jnp.dot(normed.astype(jnp.float32), shared_gate_up[1].astype(jnp.float32), preferred_element_type=jnp.float32)
    shared_act = (jax.nn.silu(shared_gate_half) * shared_up_half).astype(jnp.bfloat16)
    shared_branch = jnp.dot(shared_act.astype(jnp.float32), shared_down.astype(jnp.float32), preferred_element_type=jnp.float32)
    shared_scale = jax.nn.sigmoid(jnp.dot(normed.astype(jnp.float32), shared_gate, precision=exact_result))
    moe_sum = weighted + shared_scale[:, None] * shared_branch
    return (hidden.astype(jnp.bfloat16), moe_sum.astype(jnp.bfloat16))
```

```python
import functools

import jax
import jax.numpy as jnp
from jax import lax
from jax.experimental import pallas as pl
from jax.experimental.pallas import tpu as pltpu
from jax.sharding import PartitionSpec as P

exact = lax.Precision.HIGHEST
f32 = jnp.float32
bf16 = jnp.bfloat16
RIM = 8


def dot(a, b, dims=((1,), (0,))):
    return lax.dot_general(
        a.astype(bf16), b.astype(bf16), (dims, ((), ())), preferred_element_type=f32
    )


def dot_exact(a, b, dims=((1,), (0,))):
    return lax.dot_general(a, b, (dims, ((), ())), precision=exact, preferred_element_type=f32)


def silu(x):
    return x * jax.nn.sigmoid(x)


def shifted(value, axis, by):
    peers = lax.axis_size(axis)
    pairs = [(i, i + by) for i in range(peers) if 0 <= i + by < peers]
    return lax.ppermute(value, axis, pairs)


def unit_lower_inverse(lower, row, col):
    size = lower.shape[0]
    inverse = jnp.where(row == col, 1.0, jnp.where(row // 2 == col // 2, -lower, 0.0))
    span = 2
    while span < size:
        joins = (row // (2 * span) == col // (2 * span)) & (row // span != col // span)
        corner = jnp.where(joins, lower, 0.0)
        inverse = inverse - dot(dot(inverse, corner), inverse)
        span *= 2
    return inverse


def conv_silu(prev, own, taps, masks):
    length = own.shape[0]
    ext = jnp.concatenate([prev, own], axis=0).astype(f32)
    kernel_len = taps.shape[0]
    total = taps[kernel_len - 1 : kernel_len] * ext[RIM:]
    for i in range(kernel_len - 1):
        at = RIM - (kernel_len - 1) + i
        total = total + taps[i : i + 1] * (ext[at : at + length] * masks[:, i : i + 1])
    return silu(total)


def delta_kernel(
    qk_ref, v_ref, rim_ref, taps_qk_ref, taps_v_ref, decay_ref, beta_ref, cols_ref, row_ref,
    out_ref, query_ref, move_ref, add_ref,
):
    length = v_ref.shape[0]
    heads = decay_ref.shape[0]
    dim = v_ref.shape[1] // heads
    key_cols = taps_qk_ref.shape[1] // 2
    row = lax.broadcasted_iota(jnp.int32, (length, length), 0)
    col = lax.broadcasted_iota(jnp.int32, (length, length), 1)
    masks = cols_ref[...]
    doc_col = masks[:, 4:5]
    enters = masks[:, 5:6]
    doc_row = row_ref[0:1, :]
    keep = (row >= col) & (doc_col == doc_row)
    keep_f = keep.astype(f32)
    strict = jnp.where(row > col, keep_f, 0.0)
    decay = decay_ref[...]
    cum_row = dot_exact(decay, (row <= col).astype(f32))
    cum_col = dot_exact((row >= col).astype(f32), decay, ((1,), (1,)))
    beta_col = dot_exact((row == col).astype(f32), beta_ref[...], ((1,), (1,)))
    ends = (doc_col == doc_col[length - 1 : length]).astype(f32)
    eye = (row == col).astype(f32)

    def head_cols(ref, rim_at, taps_ref, at):
        return conv_silu(
            rim_ref[:, rim_at + at : rim_at + at + dim],
            ref[:, at : at + dim],
            taps_ref[:, at : at + dim],
            masks,
        )

    for j in range(heads // 2):
        q = head_cols(qk_ref, 0, taps_qk_ref, j * dim)
        k = head_cols(qk_ref, 0, taps_qk_ref, key_cols + j * dim)
        q = q * (lax.rsqrt(jnp.sum(q * q, axis=1, keepdims=True) + 1e-06) * dim ** (-0.5))
        k = k * lax.rsqrt(jnp.sum(k * k, axis=1, keepdims=True) + 1e-06)
        both = dot_exact(jnp.concatenate([q, k], axis=0), k, ((1,), (1,)))
        qk, kk = both[:length], both[length:]
        for h in (2 * j, 2 * j + 1):
            v = head_cols(v_ref, 2 * key_cols, taps_v_ref, h * dim)
            spread = cum_col[:, h : h + 1] - cum_row[h : h + 1, :]
            within = jnp.exp(jnp.where(keep, spread, 0.0)) * keep_f
            carried = jnp.exp(cum_col[:, h : h + 1]) * enters
            beta = beta_col[:, h : h + 1]
            inverse = unit_lower_inverse(beta * within * kk * strict, row, col)
            solved = dot(
                inverse, jnp.concatenate([beta * v, (beta * carried) * k], axis=1)
            ).astype(bf16)
            local = dot(qk * within, solved)
            last = cum_col[length - 1 : length, h : h + 1]
            to_end = jnp.exp((last - cum_col[:, h : h + 1]) * ends) * ends
            end = dot(to_end * k, solved, ((0,), (0,)))
            out_ref[h] = local[:, :dim]
            query_ref[h] = (carried * q - local[:, dim:]).astype(bf16)
            add_ref[h] = end[:, :dim]
            move_ref[h] = (carried[length - 1 : length] * eye - end[:, dim:]).astype(bf16)


def project_kernel(query_ref, out_ref, state_ref, z_ref, gain_ref, weight_ref, part_ref):
    heads, length, dim = out_ref.shape
    gated = []
    for h in range(heads):
        attn = out_ref[h] + dot(query_ref[h], state_ref[h])
        scale = lax.rsqrt(jnp.mean(attn * attn, axis=1, keepdims=True) + 1e-06)
        z = z_ref[:, h * dim : (h + 1) * dim].astype(f32)
        gated.append((attn * scale * gain_ref[...] * silu(z)).astype(bf16))
    part_ref[...] = dot(jnp.concatenate(gated, axis=1), weight_ref[...])


def expert_kernel(rows_ref, share_ref, up_ref, down_ref, out_ref):
    total = None
    for e in range(up_ref.shape[0]):
        gate = dot(rows_ref[...], up_ref[e, 0])
        up = dot(rows_ref[...], up_ref[e, 1])
        act = (silu(gate) * up).astype(bf16)
        term = share_ref[:, e : e + 1] * dot(act, down_ref[e])
        total = term if total is None else total + term
    out_ref[...] = total


def params(**more):
    return pltpu.CompilerParams(vmem_limit_bytes=56 * 1024 * 1024, **more)


VM = pl.BlockSpec(memory_space=pltpu.VMEM)


def shards(
    qk_proj, v_proj, z_proj, conv_qk, conv_v, decay_log, beta_gate, doc_ids, head_gain,
    out_weight, residual, post_gain, route_ids, route_weight, expert_gate_up, expert_down,
    shared_gate_up, shared_down, shared_gate,
):
    kernel_len = conv_qk.shape[0]
    length = qk_proj.shape[0]
    key_cols = qk_proj.shape[2]
    heads = decay_log.shape[0]
    dim = v_proj.shape[1] // heads
    width = residual.shape[1]
    seq_count = lax.axis_size("seq")
    place = lax.axis_index("seq")
    me = place * lax.axis_size("exp") + lax.axis_index("exp")
    exp_dev = expert_down.shape[0]

    own_share = jnp.sum(
        jnp.where(
            route_ids[:, :, None] == jnp.arange(exp_dev * seq_count * lax.axis_size("exp")),
            route_weight[:, :, None],
            0.0,
        ),
        axis=1,
    )
    shares = lax.all_gather(own_share, ("seq", "exp"), axis=0, tiled=True)
    shares = lax.dynamic_slice_in_dim(shares, me * exp_dev, exp_dev, axis=1)

    flat_qk = qk_proj.reshape(length, 2 * key_cols)
    rim = shifted(
        jnp.concatenate([flat_qk[length - RIM :], v_proj[length - RIM :]], axis=1), "seq", 1
    )
    pad = kernel_len - 1
    doc_pad = jnp.concatenate([jnp.full((pad,), -1, jnp.int32), doc_ids])
    window = lax.dynamic_slice_in_dim(doc_pad, place * length, length + pad)
    own_doc = window[pad:]
    cols = [(window[i : i + length] == own_doc).astype(f32) for i in range(pad)]
    cols += [jnp.zeros((length,), f32)] * (4 - pad)
    cols += [own_doc.astype(f32), (own_doc == window[pad - 1]).astype(f32)]
    cols = jnp.stack(cols, axis=1)
    out_local, query, move, add = pl.pallas_call(
        delta_kernel,
        out_shape=(
            jax.ShapeDtypeStruct((heads, length, dim), f32),
            jax.ShapeDtypeStruct((heads, length, dim), bf16),
            jax.ShapeDtypeStruct((heads, dim, dim), bf16),
            jax.ShapeDtypeStruct((heads, dim, dim), f32),
        ),
        in_specs=[VM] * 9,
        out_specs=(VM,) * 4,
        compiler_params=params(),
        name="delta",
    )(
        flat_qk, v_proj, rim, conv_qk.reshape(kernel_len, 2 * key_cols), conv_v, decay_log,
        beta_gate, cols, own_doc.astype(f32).reshape(1, length),
    )
    state = add
    for _ in range(max(1, seq_count // 4) - 1):
        before = shifted(state.astype(bf16), "seq", 1)
        state = add + jnp.einsum("hkl,hlv->hkv", move, before, preferred_element_type=f32)
    start = shifted(state.astype(bf16), "seq", 1)
    part = pl.pallas_call(
        project_kernel,
        out_shape=jax.ShapeDtypeStruct((length, width), f32),
        in_specs=[VM] * 6,
        out_specs=VM,
        compiler_params=params(),
        name="project",
    )(query, out_local, start, z_proj, head_gain.reshape(1, dim), out_weight)
    attn_part = lax.psum_scatter(part, "exp", scatter_dimension=0, tiled=True)
    hidden = residual.astype(f32) + attn_part
    normed = (
        hidden * lax.rsqrt(jnp.mean(hidden * hidden, axis=-1, keepdims=True) + 1e-06) * post_gain
    ).astype(bf16)
    gathered = lax.all_gather(normed, ("seq", "exp"), axis=0, tiled=True)
    tokens = gathered.shape[0]
    tile = 256
    parts = pl.pallas_call(
        expert_kernel,
        out_shape=jax.ShapeDtypeStruct((tokens, width), f32),
        grid=(tokens // tile,),
        in_specs=[
            pl.BlockSpec((tile, width), lambda i: (i, 0)),
            pl.BlockSpec((tile, exp_dev), lambda i: (i, 0)),
            pl.BlockSpec(expert_gate_up.shape, lambda i: (0, 0, 0, 0)),
            pl.BlockSpec(expert_down.shape, lambda i: (0, 0, 0)),
        ],
        out_specs=pl.BlockSpec((tile, width), lambda i: (i, 0)),
        compiler_params=params(),
        name="experts",
    )(gathered, shares, expert_gate_up, expert_down)
    weighted = lax.psum_scatter(parts, ("seq", "exp"), scatter_dimension=0, tiled=True)
    shared_both = jnp.einsum("rd,zdf->zrf", normed, shared_gate_up, preferred_element_type=f32)
    shared_act = (silu(shared_both[0]) * shared_both[1]).astype(bf16)
    shared_branch = jnp.dot(shared_act, shared_down, preferred_element_type=f32)
    shared_scale = jax.nn.sigmoid(jnp.dot(normed.astype(f32), shared_gate, precision=exact))
    moe_sum = weighted + shared_scale[:, None] * shared_branch
    return (hidden.astype(bf16), moe_sum.astype(bf16))


def solution(mesh):
    placed = (
        P("seq", None, "exp"),
        P("seq", "exp"),
        P("seq", "exp"),
        P(None, None, "exp"),
        P(None, "exp"),
        P("exp", "seq"),
        P("exp", "seq"),
        P(),
        P(),
        P("exp", None),
        P(("seq", "exp"), None),
        P(),
        P(("seq", "exp"), None),
        P(("seq", "exp"), None),
        P(("seq", "exp"), None, None, None),
        P(("seq", "exp"), None, None),
        P(),
        P(),
        P(),
    )
    return jax.shard_map(
        shards,
        mesh=mesh,
        in_specs=placed,
        out_specs=(P(("seq", "exp"), None), P(("seq", "exp"), None)),
        check_vma=False,
    )
```

```python
import functools

import jax
import jax.numpy as jnp
from jax import lax
from jax.experimental import pallas as pl
from jax.experimental.pallas import tpu as pltpu
from jax.sharding import PartitionSpec as P

exact = lax.Precision.HIGHEST
f32 = jnp.float32
bf16 = jnp.bfloat16
RIM = 8


def dot(a, b, dims=((1,), (0,))):
    return lax.dot_general(
        a.astype(bf16), b.astype(bf16), (dims, ((), ())), preferred_element_type=f32
    )


def dot_exact(a, b, dims=((1,), (0,))):
    return lax.dot_general(a, b, (dims, ((), ())), precision=exact, preferred_element_type=f32)


def silu(x):
    return x * jax.nn.sigmoid(x)


def shifted(value, axis, by):
    peers = lax.axis_size(axis)
    pairs = [(i, i + by) for i in range(peers) if 0 <= i + by < peers]
    return lax.ppermute(value, axis, pairs)


def unit_lower_inverse(lower, row, col):
    size = lower.shape[0]
    inverse = jnp.where(row == col, 1.0, jnp.where(row // 2 == col // 2, -lower, 0.0))
    span = 2
    while span < size:
        joins = (row // (2 * span) == col // (2 * span)) & (row // span != col // span)
        corner = jnp.where(joins, lower, 0.0)
        inverse = inverse - dot(dot(inverse, corner), inverse)
        span *= 2
    return inverse


def conv_silu(prev, own, taps, masks):
    length = own.shape[0]
    ext = jnp.concatenate([prev, own], axis=0).astype(f32)
    kernel_len = taps.shape[0]
    total = taps[kernel_len - 1 : kernel_len] * ext[RIM:]
    for i in range(kernel_len - 1):
        at = RIM - (kernel_len - 1) + i
        total = total + taps[i : i + 1] * (ext[at : at + length] * masks[:, i : i + 1])
    return silu(total)


def delta_kernel(
    qk_ref, v_ref, rim_ref, taps_qk_ref, taps_v_ref, decay_ref, beta_ref, cols_ref, row_ref,
    out_ref, query_ref, move_ref, add_ref,
):
    length = v_ref.shape[0]
    heads = decay_ref.shape[0]
    dim = v_ref.shape[1] // heads
    key_cols = taps_qk_ref.shape[1] // 2
    row = lax.broadcasted_iota(jnp.int32, (length, length), 0)
    col = lax.broadcasted_iota(jnp.int32, (length, length), 1)
    masks = cols_ref[...]
    doc_col = masks[:, 4:5]
    enters = masks[:, 5:6]
    doc_row = row_ref[0:1, :]
    keep = (row >= col) & (doc_col == doc_row)
    keep_f = keep.astype(f32)
    strict = jnp.where(row > col, keep_f, 0.0)
    decay = decay_ref[...]
    cum_row = dot_exact(decay, (row <= col).astype(f32))
    cum_col = dot_exact((row >= col).astype(f32), decay, ((1,), (1,)))
    beta_col = dot_exact((row == col).astype(f32), beta_ref[...], ((1,), (1,)))
    ends = (doc_col == doc_col[length - 1 : length]).astype(f32)
    eye = (row == col).astype(f32)

    def head_cols(ref, rim_at, taps_ref, at):
        return conv_silu(
            rim_ref[:, rim_at + at : rim_at + at + dim],
            ref[:, at : at + dim],
            taps_ref[:, at : at + dim],
            masks,
        )

    for j in range(heads // 2):
        q = head_cols(qk_ref, 0, taps_qk_ref, j * dim)
        k = head_cols(qk_ref, 0, taps_qk_ref, key_cols + j * dim)
        q = q * (lax.rsqrt(jnp.sum(q * q, axis=1, keepdims=True) + 1e-06) * dim ** (-0.5))
        k = k * lax.rsqrt(jnp.sum(k * k, axis=1, keepdims=True) + 1e-06)
        both = dot_exact(jnp.concatenate([q, k], axis=0), k, ((1,), (1,)))
        qk, kk = both[:length], both[length:]
        for h in (2 * j, 2 * j + 1):
            v = head_cols(v_ref, 2 * key_cols, taps_v_ref, h * dim)
            spread = cum_col[:, h : h + 1] - cum_row[h : h + 1, :]
            within = jnp.exp(jnp.where(keep, spread, 0.0)) * keep_f
            carried = jnp.exp(cum_col[:, h : h + 1]) * enters
            beta = beta_col[:, h : h + 1]
            inverse = unit_lower_inverse(beta * within * kk * strict, row, col)
            solved = dot(
                inverse, jnp.concatenate([beta * v, (beta * carried) * k], axis=1)
            ).astype(bf16)
            local = dot(qk * within, solved)
            last = cum_col[length - 1 : length, h : h + 1]
            to_end = jnp.exp((last - cum_col[:, h : h + 1]) * ends) * ends
            end = dot(to_end * k, solved, ((0,), (0,)))
            out_ref[h] = local[:, :dim]
            query_ref[h] = (carried * q - local[:, dim:]).astype(bf16)
            add_ref[h] = end[:, :dim]
            move_ref[h] = (carried[length - 1 : length] * eye - end[:, dim:]).astype(bf16)


def project_kernel(query_ref, out_ref, state_ref, z_ref, gain_ref, weight_ref, part_ref):
    heads, length, dim = out_ref.shape
    gated = []
    for h in range(heads):
        attn = out_ref[h] + dot(query_ref[h], state_ref[h])
        scale = lax.rsqrt(jnp.mean(attn * attn, axis=1, keepdims=True) + 1e-06)
        z = z_ref[:, h * dim : (h + 1) * dim].astype(f32)
        gated.append((attn * scale * gain_ref[...] * silu(z)).astype(bf16))
    part_ref[...] = dot(jnp.concatenate(gated, axis=1), weight_ref[...])


def expert_kernel(rows_ref, share_ref, up_ref, down_ref, out_ref):
    total = None
    for e in range(up_ref.shape[0]):
        gate = dot(rows_ref[...], up_ref[e, 0])
        up = dot(rows_ref[...], up_ref[e, 1])
        act = (silu(gate) * up).astype(bf16)
        term = share_ref[:, e : e + 1] * dot(act, down_ref[e])
        total = term if total is None else total + term
    out_ref[...] = total


def params(**more):
    return pltpu.CompilerParams(vmem_limit_bytes=56 * 1024 * 1024, **more)


MESH = pl.DeviceIdType.MESH


def moe_kernel(
    query_ref, local_ref, state_ref, z_ref, head_gain_ref, residual_ref, post_gain_ref, share_ref,
    gate_ref, weight_hbm, up_hbm, down_hbm, shared_up_hbm, shared_down_hbm,
    hidden_ref, moe_ref,
    weight, up, down, shared_up, shared_down, part, part_send, part_recv, tok, mine, core_send,
    core_recv, pass_x, pass_y, send_x, send_y, recv_x, recv_y, back_send, back_recv,
    load_sem, part_sems, tok_sems, core_sems, plane_sems, back_sems,
):
    heads, length, dim = local_ref.shape
    rows, width = residual_ref.shape
    depth = length // rows
    seq = lax.axis_index("seq")
    z = lax.axis_index("exp")
    core = lax.rem(seq, 2)
    x = lax.rem(seq // 2, 2)
    y = seq // 4
    to_core = (seq + 1 - 2 * core, z)
    to_x = (seq + 2 - 4 * x, z)
    to_y = (seq + 4 - 8 * y, z)
    ahead = [(seq, lax.rem(z + k, depth)) for k in range(depth)]

    loads = []
    for n, (src, dst) in enumerate(
        ((weight_hbm, weight), (shared_up_hbm, shared_up), (shared_down_hbm, shared_down),
         (up_hbm, up), (down_hbm, down))
    ):
        load = pltpu.make_async_copy(src, dst, load_sem.at[n])
        load.start()
        loads.append(load)

    barrier = pltpu.get_barrier_semaphore()
    peers = [to_core, to_x, to_y] + ahead[1:]
    for peer in peers:
        pl.semaphore_signal(barrier, inc=1, device_id=peer, device_id_type=MESH)
    pl.semaphore_wait(barrier, len(peers))

    def send(src, dst, sems, at, peer):
        copy = pltpu.make_async_remote_copy(
            src_ref=src, dst_ref=dst, send_sem=sems.at[0, at], recv_sem=sems.at[1, at],
            device_id=peer, device_id_type=MESH,
        )
        copy.start()
        return copy

    gated = []
    for h in range(heads):
        attn = local_ref[h] + dot(query_ref[h], state_ref[h])
        scale = lax.rsqrt(jnp.mean(attn * attn, axis=1, keepdims=True) + 1e-06)
        gate_z = z_ref[:, h * dim : (h + 1) * dim].astype(f32)
        gated.append((attn * scale * head_gain_ref[...] * silu(gate_z)).astype(bf16))
    gated = jnp.concatenate(gated, axis=1)
    loads[0].wait()
    tile = width // 4
    for n in range(0, width, tile):
        product = dot(gated, weight[:, n : n + tile])
        part[:, n : n + tile] = product
        part_send[:, n : n + tile] = product.astype(bf16)

    def block_rows(k):
        return pl.ds(pl.multiple_of(lax.rem(z + k, depth) * rows, rows), rows)

    part_copies = {}
    for k in range(depth - 1, 0, -1):
        back = depth - k
        part_copies[k] = send(
            part_send.at[block_rows(k)], part_recv.at[back], part_sems, back, ahead[k]
        )
    hidden = residual_ref[...].astype(f32) + part[block_rows(0), :]
    for k in range(1, depth):
        part_copies[k].wait()
    for k in range(1, depth):
        hidden = hidden + part_recv[k].astype(f32)
    hidden_ref[...] = hidden.astype(bf16)
    normed = (
        hidden * lax.rsqrt(jnp.mean(hidden * hidden, axis=1, keepdims=True) + 1e-06)
        * post_gain_ref[...]
    ).astype(bf16)
    tok[0, :, 0:width] = normed
    tok[0, :, width:] = share_ref[...]

    def slot(group, other, k):
        return (group * 2 + other) * depth + k

    copies = []

    def pass_on(at, to, peer):
        copies.append(send(tok.at[at], tok.at[to], tok_sems, to, peer))

    def arrived(at):
        pltpu.make_async_remote_copy(
            src_ref=tok.at[at], dst_ref=tok.at[at], send_sem=tok_sems.at[0, at],
            recv_sem=tok_sems.at[1, at], device_id=to_core, device_id_type=MESH,
        ).wait_recv()

    def spread_own(k):
        pass_on(slot(0, 0, k), slot(1, 0, k), to_x)
        pass_on(slot(0, 0, k), slot(2, 0, k), to_y)
        pass_on(slot(0, 0, k), slot(0, 1, k), to_core)

    for k in range(1, depth):
        pass_on(0, slot(0, 0, depth - k), ahead[k])
    spread_own(0)
    score = jax.nn.sigmoid(
        jnp.sum(normed.astype(f32) * gate_ref[...], axis=1, keepdims=True)
    )
    loads[1].wait()
    shared_gate = dot(normed, shared_up[0])
    arrived(slot(0, 0, 1))
    spread_own(1)
    shared_act = (silu(shared_gate) * dot(normed, shared_up[1])).astype(bf16)
    arrived(slot(0, 0, depth - 1))
    spread_own(depth - 1)
    loads[2].wait()
    moe = score * dot(shared_act, shared_down[...])
    for k in range(2, depth - 1):
        arrived(slot(0, 0, k))
        spread_own(k)
    loads[3].wait()
    loads[4].wait()

    experts = up.shape[0]
    lanes = tok.shape[2] - width
    first = (seq * depth + z) * experts
    lane = lax.broadcasted_iota(jnp.int32, (1, lanes), 1)
    lane = lax.rem(lane, lanes // 2)
    half = depth * rows
    core_copies = {}

    def work(group):
        at = slot(group, 0, 0)
        both = 2 * depth
        held = tok[at : at + both, :, 0:width].reshape(both * rows, width)
        shares = tok[at : at + both, :, width:].reshape(both * rows, lanes).astype(f32)
        acts = []
        for e in range(experts):
            gate = dot(held, up[e, 0])
            acts.append((silu(gate) * dot(held, up[e, 1])).astype(bf16))
        share = [
            jnp.sum(jnp.where(lane == first + e, shares, 0.0), axis=1, keepdims=True)
            for e in range(experts)
        ]
        for n in range(0, width, tile):
            total = share[0] * dot(acts[0], down[0, :, n : n + tile])
            for e in range(1, experts):
                total = total + share[e] * dot(acts[e], down[e, :, n : n + tile])
            mine[group, :, n : n + tile] = total[:half]
            core_send[group, :, n : n + tile] = total[half:]
        core_copies[group] = send(
            core_send.at[group], core_recv.at[group], core_sems, group, to_core
        )

    for k in range(depth):
        arrived(slot(0, 1, k))
    work(0)
    middle = depth // 2
    for k in range(depth):
        arrived(slot(1, 0, k))
        pass_on(slot(1, 0, k), slot(1, 1, k), to_core)
        if k < middle:
            pass_on(slot(1, 0, k), slot(3, 0, k), to_y)
        arrived(slot(2, 0, k))
        pass_on(slot(2, 0, k), slot(2, 1, k), to_core)
        if k >= middle:
            pass_on(slot(2, 0, k), slot(3, 0, k), to_x)
    for k in range(depth):
        arrived(slot(1, 1, k))
    work(1)
    for k in range(depth):
        arrived(slot(3, 0, k))
        pass_on(slot(3, 0, k), slot(3, 1, k), to_core)
    for k in range(depth):
        arrived(slot(2, 1, k))
    work(2)
    cut = middle * rows
    low, high = slice(0, cut), slice(cut, half)
    core_copies[1].wait()
    send_x[0] = (mine[1, low, :] + core_recv[1, low, :]).astype(bf16)
    plane = [send(send_x.at[0], recv_x.at[0], plane_sems, 0, to_x)]
    core_copies[2].wait()
    send_y[1] = (mine[2, high, :] + core_recv[2, high, :]).astype(bf16)
    plane.append(send(send_y.at[1], recv_y.at[1], plane_sems, 1, to_y))
    for k in range(depth):
        arrived(slot(3, 1, k))
    work(3)
    core_copies[3].wait()
    send_x[2] = (mine[3, low, :] + core_recv[3, low, :]).astype(bf16)
    by_x = send(send_x.at[2], pass_x, plane_sems, 2, to_x)
    send_y[2] = (mine[3, high, :] + core_recv[3, high, :]).astype(bf16)
    by_y = send(send_y.at[2], pass_y, plane_sems, 3, to_y)
    core_copies[0].wait()
    own = mine[0] + core_recv[0]
    mine[0] = own
    by_x.wait()
    send_y[0] = (mine[2, low, :] + core_recv[2, low, :] + pass_x[...].astype(f32)).astype(bf16)
    plane.append(send(send_y.at[0], recv_y.at[0], plane_sems, 4, to_y))
    by_y.wait()
    send_x[1] = (mine[1, high, :] + core_recv[1, high, :] + pass_y[...].astype(f32)).astype(bf16)
    plane.append(send(send_x.at[1], recv_x.at[1], plane_sems, 5, to_x))
    for copy in plane:
        copy.wait()
    back_copies = []

    def summed(k):
        part_at, at = k // middle, k % middle * rows
        return (
            mine[0, k * rows : (k + 1) * rows, :]
            + recv_x[part_at, at : at + rows, :].astype(f32)
            + recv_y[part_at, at : at + rows, :].astype(f32)
        )

    for k in range(1, depth):
        back_send[k] = summed(k).astype(bf16)
        back_copies.append(
            send(back_send.at[k], back_recv.at[depth - k], back_sems, depth - k, ahead[k])
        )
    moe = moe + summed(0)
    for copy in back_copies:
        copy.wait()
    for k in range(1, depth):
        moe = moe + back_recv[k].astype(f32)
    moe_ref[...] = moe.astype(bf16)
    for copy in copies:
        copy.wait_send()


def moe_call(
    query, out_local, start, z_proj, head_gain, residual, post_gain, share, shared_gate,
    out_weight, expert_gate_up, expert_down, shared_gate_up, shared_down,
):
    heads, length, dim = out_local.shape
    rows, width = residual.shape
    depth = length // rows
    half, cut = depth * rows, depth // 2 * rows
    row_block = jax.ShapeDtypeStruct((rows, width), bf16)
    anywhere = pl.BlockSpec(memory_space=pl.ANY)
    dma = pltpu.SemaphoreType.DMA
    return pl.pallas_call(
        moe_kernel,
        out_shape=(row_block, row_block),
        in_specs=[VM] * 9 + [anywhere] * 5,
        out_specs=(VM, VM),
        scratch_shapes=[
            pltpu.VMEM(out_weight.shape, bf16),
            pltpu.VMEM(expert_gate_up.shape, bf16),
            pltpu.VMEM(expert_down.shape, bf16),
            pltpu.VMEM(shared_gate_up.shape, bf16),
            pltpu.VMEM(shared_down.shape, bf16),
            pltpu.VMEM((length, width), f32),
            pltpu.VMEM((length, width), bf16),
            pltpu.VMEM((depth, rows, width), bf16),
            pltpu.VMEM((8 * depth, rows, width + share.shape[1]), bf16),
            pltpu.VMEM((4, half, width), f32),
            pltpu.VMEM((4, half, width), f32),
            pltpu.VMEM((4, half, width), f32),
            pltpu.VMEM((cut, width), bf16),
            pltpu.VMEM((cut, width), bf16),
            pltpu.VMEM((3, cut, width), bf16),
            pltpu.VMEM((3, cut, width), bf16),
            pltpu.VMEM((2, cut, width), bf16),
            pltpu.VMEM((2, cut, width), bf16),
            pltpu.VMEM((depth, rows, width), bf16),
            pltpu.VMEM((depth, rows, width), bf16),
            dma((5,)),
            dma((2, depth)),
            dma((2, 8 * depth)),
            dma((2, 4)),
            dma((2, 6)),
            dma((2, depth)),
        ],
        compiler_params=params(collective_id=1, has_side_effects=True),
        name="moe",
    )(
        query, out_local, start, z_proj, head_gain.reshape(1, dim), residual,
        post_gain.reshape(1, width), share, shared_gate.reshape(1, width), out_weight,
        expert_gate_up, expert_down, shared_gate_up, shared_down,
    )


VM = pl.BlockSpec(memory_space=pltpu.VMEM)


def shards(
    qk_proj, v_proj, z_proj, conv_qk, conv_v, decay_log, beta_gate, doc_ids, head_gain,
    out_weight, residual, post_gain, route_ids, route_weight, expert_gate_up, expert_down,
    shared_gate_up, shared_down, shared_gate,
):
    kernel_len = conv_qk.shape[0]
    length = qk_proj.shape[0]
    key_cols = qk_proj.shape[2]
    heads = decay_log.shape[0]
    dim = v_proj.shape[1] // heads
    width = residual.shape[1]
    seq_count = lax.axis_size("seq")
    place = lax.axis_index("seq")
    me = place * lax.axis_size("exp") + lax.axis_index("exp")
    exp_dev = expert_down.shape[0]

    own_share = jnp.sum(
        jnp.where(
            route_ids[:, :, None] == jnp.arange(exp_dev * seq_count * lax.axis_size("exp")),
            route_weight[:, :, None],
            0.0,
        ),
        axis=1,
    )
    flat_qk = qk_proj.reshape(length, 2 * key_cols)
    rim = shifted(
        jnp.concatenate([flat_qk[length - RIM :], v_proj[length - RIM :]], axis=1), "seq", 1
    )
    pad = kernel_len - 1
    doc_pad = jnp.concatenate([jnp.full((pad,), -1, jnp.int32), doc_ids])
    window = lax.dynamic_slice_in_dim(doc_pad, place * length, length + pad)
    own_doc = window[pad:]
    cols = [(window[i : i + length] == own_doc).astype(f32) for i in range(pad)]
    cols += [jnp.zeros((length,), f32)] * (4 - pad)
    cols += [own_doc.astype(f32), (own_doc == window[pad - 1]).astype(f32)]
    cols = jnp.stack(cols, axis=1)
    out_local, query, move, add = pl.pallas_call(
        delta_kernel,
        out_shape=(
            jax.ShapeDtypeStruct((heads, length, dim), f32),
            jax.ShapeDtypeStruct((heads, length, dim), bf16),
            jax.ShapeDtypeStruct((heads, dim, dim), bf16),
            jax.ShapeDtypeStruct((heads, dim, dim), f32),
        ),
        in_specs=[VM] * 9,
        out_specs=(VM,) * 4,
        compiler_params=params(),
        name="delta",
    )(
        flat_qk, v_proj, rim, conv_qk.reshape(kernel_len, 2 * key_cols), conv_v, decay_log,
        beta_gate, cols, own_doc.astype(f32).reshape(1, length),
    )
    state = add
    for _ in range(max(1, seq_count // 4) - 1):
        before = shifted(state.astype(bf16), "seq", 1)
        state = add + jnp.einsum("hkl,hlv->hkv", move, before, preferred_element_type=f32)
    start = shifted(state.astype(bf16), "seq", 1)
    if seq_count == 8 and lax.axis_size("exp") == 4 and 2 * own_share.shape[1] == 128:
        rounded = own_share.astype(bf16)
        rest = (own_share - rounded.astype(f32)).astype(bf16)
        share = jnp.concatenate([rounded, rest], axis=1)
        return moe_call(
            query, out_local, start, z_proj, head_gain, residual, post_gain, share, shared_gate,
            out_weight, expert_gate_up, expert_down, shared_gate_up, shared_down,
        )
    shares = lax.all_gather(own_share, ("seq", "exp"), axis=0, tiled=True)
    shares = lax.dynamic_slice_in_dim(shares, me * exp_dev, exp_dev, axis=1)
    part = pl.pallas_call(
        project_kernel,
        out_shape=jax.ShapeDtypeStruct((length, width), f32),
        in_specs=[VM] * 6,
        out_specs=VM,
        compiler_params=params(),
        name="project",
    )(query, out_local, start, z_proj, head_gain.reshape(1, dim), out_weight)
    attn_part = lax.psum_scatter(part, "exp", scatter_dimension=0, tiled=True)
    hidden = residual.astype(f32) + attn_part
    normed = (
        hidden * lax.rsqrt(jnp.mean(hidden * hidden, axis=-1, keepdims=True) + 1e-06) * post_gain
    ).astype(bf16)
    gathered = lax.all_gather(normed, ("seq", "exp"), axis=0, tiled=True)
    tokens = gathered.shape[0]
    tile = 256
    parts = pl.pallas_call(
        expert_kernel,
        out_shape=jax.ShapeDtypeStruct((tokens, width), f32),
        grid=(tokens // tile,),
        in_specs=[
            pl.BlockSpec((tile, width), lambda i: (i, 0)),
            pl.BlockSpec((tile, exp_dev), lambda i: (i, 0)),
            pl.BlockSpec(expert_gate_up.shape, lambda i: (0, 0, 0, 0)),
            pl.BlockSpec(expert_down.shape, lambda i: (0, 0, 0)),
        ],
        out_specs=pl.BlockSpec((tile, width), lambda i: (i, 0)),
        compiler_params=params(),
        name="experts",
    )(gathered, shares, expert_gate_up, expert_down)
    weighted = lax.psum_scatter(parts, ("seq", "exp"), scatter_dimension=0, tiled=True)
    shared_both = jnp.einsum("rd,zdf->zrf", normed, shared_gate_up, preferred_element_type=f32)
    shared_act = (silu(shared_both[0]) * shared_both[1]).astype(bf16)
    shared_branch = jnp.dot(shared_act, shared_down, preferred_element_type=f32)
    shared_scale = jax.nn.sigmoid(jnp.dot(normed.astype(f32), shared_gate, precision=exact))
    moe_sum = weighted + shared_scale[:, None] * shared_branch
    return (hidden.astype(bf16), moe_sum.astype(bf16))


def solution(mesh):
    placed = (
        P("seq", None, "exp"),
        P("seq", "exp"),
        P("seq", "exp"),
        P(None, None, "exp"),
        P(None, "exp"),
        P("exp", "seq"),
        P("exp", "seq"),
        P(),
        P(),
        P("exp", None),
        P(("seq", "exp"), None),
        P(),
        P(("seq", "exp"), None),
        P(("seq", "exp"), None),
        P(("seq", "exp"), None, None, None),
        P(("seq", "exp"), None, None),
        P(),
        P(),
        P(),
    )
    return jax.shard_map(
        shards,
        mesh=mesh,
        in_specs=placed,
        out_specs=(P(("seq", "exp"), None), P(("seq", "exp"), None)),
        check_vma=False,
    )
```

```python
import functools

import jax
import jax.numpy as jnp
from jax import lax
from jax.experimental import pallas as pl
from jax.experimental.pallas import tpu as pltpu
from jax.sharding import PartitionSpec as P

exact = lax.Precision.HIGHEST
f32 = jnp.float32
bf16 = jnp.bfloat16
RIM = 16


def dot(a, b, dims=((1,), (0,))):
    return lax.dot_general(
        a.astype(bf16), b.astype(bf16), (dims, ((), ())), preferred_element_type=f32
    )


def dot_exact(a, b, dims=((1,), (0,))):
    return lax.dot_general(a, b, (dims, ((), ())), precision=exact, preferred_element_type=f32)


def silu(x):
    return x * jax.nn.sigmoid(x)


def shifted(value, axis, by):
    peers = lax.axis_size(axis)
    pairs = [(i, i + by) for i in range(peers) if 0 <= i + by < peers]
    return lax.ppermute(value, axis, pairs)


def dot_split(a, b, dims=((1,), (0,))):
    a_low = a - a.astype(bf16).astype(f32)
    b_low = b - b.astype(bf16).astype(f32)
    return dot(a, b, dims) + (dot(a_low, b, dims) + dot(a, b_low, dims))


def unit_lower_inverses(lowers, row, col):
    size = lowers[0].shape[0]
    inverses = [
        jnp.where(row == col, 1.0, jnp.where(row // 2 == col // 2, -lower, 0.0))
        for lower in lowers
    ]
    span = 2
    while span < size:
        joins = (row // (2 * span) == col // (2 * span)) & (row // span != col // span)
        corners = [
            dot(inverse, jnp.where(joins, lower, 0.0))
            for inverse, lower in zip(inverses, lowers)
        ]
        inverses = [
            inverse - dot(corner, inverse) for inverse, corner in zip(inverses, corners)
        ]
        span *= 2
    return inverses


def conv_silu(prev, own, taps, masks):
    length = own.shape[0]
    ext = jnp.concatenate([prev, own], axis=0).astype(f32)
    total = taps[-1] * ext[RIM:]
    for i in range(len(taps) - 1):
        at = RIM - (len(taps) - 1) + i
        total = total + taps[i] * (ext[at : at + length] * masks[i])
    return silu(total)


def delta_body(
    conv_key, conv_value, decay, beta, doc_col, doc_row, enters, out_ref, query_ref, move_ref,
    add_ref, after,
):
    length = doc_row.shape[1]
    heads, _, dim = add_ref.shape
    row = lax.broadcasted_iota(jnp.int32, (length, length), 0)
    col = lax.broadcasted_iota(jnp.int32, (length, length), 1)
    keep = (row >= col) & (doc_col == doc_row)
    keep_f = keep.astype(f32)
    strict = jnp.where(row > col, keep_f, 0.0)
    eye = (row == col).astype(f32)
    cum_row = dot_exact(decay, (row <= col).astype(f32))
    cum_col = dot_exact((row >= col).astype(f32), decay, ((1,), (1,)))
    beta_col = dot_exact(eye, beta, ((1,), (1,)))
    ends = (doc_col == doc_col[length - 1 : length]).astype(f32)
    batch = 4 if heads % 4 == 0 else 2
    for first in range(0, heads, batch):
        group = range(first, first + batch)
        q, k, qk, kk = {}, {}, {}, {}
        for j in range(first // 2, (first + batch) // 2):
            qj, kj = conv_key(0, j), conv_key(1, j)
            q[j] = qj * (lax.rsqrt(jnp.sum(qj * qj, axis=1, keepdims=True) + 1e-06) * dim ** (-0.5))
            k[j] = kj * lax.rsqrt(jnp.sum(kj * kj, axis=1, keepdims=True) + 1e-06)
            both = dot_exact(jnp.concatenate([q[j], k[j]], axis=0), k[j], ((1,), (1,)))
            qk[j], kk[j] = both[:length], both[length:]
        within, carried, lowers = [], [], []
        for h in group:
            spread = cum_col[:, h : h + 1] - cum_row[h : h + 1, :]
            within.append(jnp.exp(jnp.where(keep, spread, 0.0)) * keep_f)
            carried.append(jnp.exp(cum_col[:, h : h + 1]) * enters)
            lowers.append(beta_col[:, h : h + 1] * within[-1] * kk[h // 2] * strict)
        inverses = unit_lower_inverses(lowers, row, col)
        solved = []
        for n, h in enumerate(group):
            b = beta_col[:, h : h + 1]
            sides = jnp.concatenate([b * conv_value(h), (b * carried[n]) * k[h // 2]], axis=1)
            solved.append(dot_split(inverses[n], sides))
        for n, h in enumerate(group):
            last = cum_col[length - 1 : length, h : h + 1]
            to_end = jnp.exp((last - cum_col[:, h : h + 1]) * ends) * ends
            end = dot(to_end * k[h // 2], solved[n], ((0,), (0,)))
            add_ref[h] = end[:, :dim]
            move_ref[h] = (carried[n][length - 1 : length] * eye - end[:, dim:]).astype(bf16)
        after(first, batch)
        for n, h in enumerate(group):
            local = dot_split(qk[h // 2] * within[n], solved[n])
            out_ref[h] = local[:, :dim]
            query_ref[h] = (carried[n] * q[h // 2] - local[:, dim:]).astype(bf16)


def delta_kernel(
    qk_ref, v_ref, rim_ref, taps_qk_ref, taps_v_ref, decay_ref, beta_ref, cols_ref, row_ref,
    out_ref, query_ref, move_ref, add_ref,
):
    dim = add_ref.shape[1]
    key_cols = taps_qk_ref.shape[1] // 2
    kernel_len = taps_v_ref.shape[0]
    cols = cols_ref[...]
    masks = [cols[:, i : i + 1] for i in range(kernel_len - 1)]

    def head(ref, rim_at, taps_ref, at):
        taps = [taps_ref[i : i + 1, at : at + dim] for i in range(kernel_len)]
        rim = rim_ref[:, rim_at + at : rim_at + at + dim]
        return conv_silu(rim, ref[:, at : at + dim], taps, masks)

    delta_body(
        lambda half, j: head(qk_ref, 0, taps_qk_ref, half * key_cols + j * dim),
        lambda h: head(v_ref, 2 * key_cols, taps_v_ref, h * dim),
        decay_ref[...], beta_ref[...], cols[:, 4:5], row_ref[0:1, :], cols[:, 5:6],
        out_ref, query_ref, move_ref, add_ref, lambda first, batch: None,
    )


def project_kernel(query_ref, out_ref, state_ref, z_ref, gain_ref, weight_ref, part_ref):
    heads, length, dim = out_ref.shape
    gated = []
    for h in range(heads):
        attn = out_ref[h] + dot(query_ref[h], state_ref[h])
        scale = lax.rsqrt(jnp.mean(attn * attn, axis=1, keepdims=True) + 1e-06)
        z = z_ref[:, h * dim : (h + 1) * dim].astype(f32)
        gated.append((attn * scale * gain_ref[...] * silu(z)).astype(bf16))
    part_ref[...] = dot(jnp.concatenate(gated, axis=1), weight_ref[...])


def expert_kernel(rows_ref, share_ref, up_ref, down_ref, out_ref):
    total = None
    for e in range(up_ref.shape[0]):
        gate = dot(rows_ref[...], up_ref[e, 0])
        up = dot(rows_ref[...], up_ref[e, 1])
        act = (silu(gate) * up).astype(bf16)
        term = share_ref[:, e : e + 1] * dot(act, down_ref[e])
        total = term if total is None else total + term
    out_ref[...] = total


def params(**more):
    return pltpu.CompilerParams(vmem_limit_bytes=56 * 1024 * 1024, **more)


MESH = pl.DeviceIdType.MESH


def moe_kernel(
    qk_ref, v_ref, taps_qk_ref, taps_v_ref, decay_ref, beta_ref, doc_ref, ids_ref, route_ref,
    z_ref, head_gain_ref, residual_ref, post_gain_ref, gate_ref, weight_hbm, up_hbm, down_hbm, shared_up_hbm, shared_down_hbm,
    hidden_ref, moe_ref,
    rim_qk, rim_v, local_ref, query_ref, move, add, add_send, add_recv, state_send, state_recv,
    weight, up, down, shared_up, shared_down, part, part_send, part_recv, tok, mine, core_send,
    core_recv, pass_x, pass_y, send_x, send_y, recv_x, recv_y, back_send, back_recv,
    load_sem, rim_sems, hop_sems, part_sems, tok_sems, core_sems, plane_sems, back_sems,
):
    heads, length, dim = local_ref.shape
    rows, width = residual_ref.shape
    depth = length // rows
    experts = up.shape[0]
    lanes = tok.shape[2] - width
    seq = lax.axis_index("seq")
    z = lax.axis_index("exp")
    core = lax.rem(seq, 2)
    x = lax.rem(seq // 2, 2)
    y = seq // 4
    seqs = lax.axis_size("seq")
    to_next = (lax.rem(seq + 1, seqs), z)
    to_last = (lax.rem(seq + seqs - 1, seqs), z)
    to_core = (seq + 1 - 2 * core, z)
    to_x = (seq + 2 - 4 * x, z)
    to_y = (seq + 4 - 8 * y, z)
    ahead = [(seq, lax.rem(z + k, depth)) for k in range(depth)]

    loads = []
    for n, (src, dst) in enumerate(
        ((weight_hbm, weight), (shared_up_hbm, shared_up), (shared_down_hbm, shared_down),
         (up_hbm, up), (down_hbm, down))
    ):
        load = pltpu.make_async_copy(src, dst, load_sem.at[n])
        load.start()
        loads.append(load)

    barrier = pltpu.get_barrier_semaphore()
    peers = [to_next, to_last, to_core, to_x, to_y] + ahead[1:]
    for peer in peers:
        pl.semaphore_signal(barrier, inc=1, device_id=peer, device_id_type=MESH)
    pl.semaphore_wait(barrier, len(peers))

    def send(src, dst, sems, at, peer):
        copy = pltpu.make_async_remote_copy(
            src_ref=src, dst_ref=dst, send_sem=sems.at[0, at], recv_sem=sems.at[1, at],
            device_id=peer, device_id_type=MESH,
        )
        copy.start()
        return copy

    tail = pl.ds(length - RIM, RIM)
    rims = [
        send(qk_ref.at[tail], rim_qk, rim_sems, 0, to_next),
        send(v_ref.at[tail], rim_v, rim_sems, 1, to_next),
    ]
    kernel_len = taps_v_ref.shape[0]
    doc_row = doc_ref[:, pl.ds(pl.multiple_of(seq * length, length), length)].astype(f32)
    before = jnp.maximum(seq - 1, 0)
    doc_before = doc_ref[:, pl.ds(pl.multiple_of(before * length, length), length)].astype(f32)
    doc_before = jnp.where(seq == 0, -1.0, doc_before)
    doc_both = jnp.broadcast_to(
        jnp.concatenate([doc_before, doc_row], axis=1), (8, 2 * length)
    )
    token = lax.broadcasted_iota(jnp.int32, (length, 2 * length), 0) + length
    other = lax.broadcasted_iota(jnp.int32, (length, 2 * length), 1)
    doc_cols = [
        dot_exact((other == token - i).astype(f32), doc_both, ((1,), (1,)))[:, 0:1]
        for i in range(kernel_len)
    ]
    enters = (doc_cols[0] == doc_before[:, length - 1 : length]).astype(f32)
    same = [(doc_cols[i] == doc_cols[0]).astype(f32) for i in range(kernel_len - 1, 0, -1)]

    def key_head(part_at, j):
        at = slice(j * dim, (j + 1) * dim)
        taps = [taps_qk_ref[i, part_at : part_at + 1, at] for i in range(kernel_len)]
        at = slice((part_at * heads // 2 + j) * dim, (part_at * heads // 2 + j + 1) * dim)
        return conv_silu(rim_qk[:, at], qk_ref[:, at], taps, same)

    def value_head(h):
        at = slice(h * dim, (h + 1) * dim)
        taps = [taps_v_ref[i : i + 1, at] for i in range(kernel_len)]
        return conv_silu(rim_v[:, at], v_ref[:, at], taps, same)

    hops = []

    def hop(first, batch):
        group = pl.ds(first, batch)
        add_send[group] = add[group].astype(bf16)
        at = first // batch
        copy = send(add_send.at[group], add_recv.at[group], hop_sems, at, to_next)
        hops.append((first, batch, at, copy))

    for copy in rims:
        copy.wait()
    delta_body(
        key_head, value_head, decay_ref[...], beta_ref[...], doc_cols[0], doc_row, enters,
        local_ref, query_ref, move, add, hop,
    )
    states = []
    for first, batch, at, copy in hops:
        copy.wait()
        for h in range(first, first + batch):
            state_send[h] = (add[h] + dot(move[h], add_recv[h])).astype(bf16)
        group = pl.ds(first, batch)
        states.append(
            send(
                state_send.at[group], state_recv.at[group], hop_sems, len(hops) + at, to_next
            )
        )
    gated = []
    for h in range(heads):
        if h % hops[0][1] == 0:
            states[h // hops[0][1]].wait()
        attn = local_ref[h] + dot(query_ref[h], state_recv[h])
        scale = lax.rsqrt(jnp.mean(attn * attn, axis=1, keepdims=True) + 1e-06)
        gate_z = z_ref[:, h * dim : (h + 1) * dim].astype(f32)
        gated.append((attn * scale * head_gain_ref[...] * silu(gate_z)).astype(bf16))
    gated = jnp.concatenate(gated, axis=1)
    loads[0].wait()
    tile = width // 4
    for n in range(0, width, tile):
        product = dot(gated, weight[:, n : n + tile])
        part[:, n : n + tile] = product
        part_send[:, n : n + tile] = product.astype(bf16)

    def block_rows(k):
        return pl.ds(pl.multiple_of(lax.rem(z + k, depth) * rows, rows), rows)

    part_copies = {}
    for k in range(depth - 1, 0, -1):
        back = depth - k
        part_copies[k] = send(
            part_send.at[block_rows(k)], part_recv.at[back], part_sems, back, ahead[k]
        )
    hidden = residual_ref[...].astype(f32) + part[block_rows(0), :]
    for k in range(1, depth):
        part_copies[k].wait()
    for k in range(1, depth):
        hidden = hidden + part_recv[k].astype(f32)
    hidden_ref[...] = hidden.astype(bf16)
    normed = (
        hidden * lax.rsqrt(jnp.mean(hidden * hidden, axis=1, keepdims=True) + 1e-06)
        * post_gain_ref[...]
    ).astype(bf16)
    tok[0, :, 0:width] = normed
    lane = lax.broadcasted_iota(jnp.int32, (1, lanes), 1)
    named = lax.rem(lane, lanes // 2)
    share = jnp.zeros((rows, lanes), f32)
    for n in range(ids_ref.shape[1]):
        share = share + jnp.where(ids_ref[:, n : n + 1] == named, route_ref[:, n : n + 1], 0.0)
    rest = share - share.astype(bf16).astype(f32)
    tok[0, :, width:] = jnp.where(lane < lanes // 2, share, rest).astype(bf16)

    def slot(group, other, k):
        return (group * 2 + other) * depth + k

    copies = []

    def pass_on(at, to, peer):
        copies.append(send(tok.at[at], tok.at[to], tok_sems, to, peer))

    def arrived(at):
        pltpu.make_async_remote_copy(
            src_ref=tok.at[at], dst_ref=tok.at[at], send_sem=tok_sems.at[0, at],
            recv_sem=tok_sems.at[1, at], device_id=to_core, device_id_type=MESH,
        ).wait_recv()

    def spread_own(k):
        pass_on(slot(0, 0, k), slot(1, 0, k), to_x)
        pass_on(slot(0, 0, k), slot(2, 0, k), to_y)
        pass_on(slot(0, 0, k), slot(0, 1, k), to_core)

    for k in range(1, depth):
        pass_on(0, slot(0, 0, depth - k), ahead[k])
    spread_own(0)
    for k in [1, depth - 1] + list(range(2, depth - 1)):
        arrived(slot(0, 0, k))
        spread_own(k)
    loads[3].wait()
    loads[4].wait()

    first = (seq * depth + z) * experts
    half = depth * rows
    core_copies = {}

    def work(group):
        at = slot(group, 0, 0)
        both = 2 * depth
        held = tok[at : at + both, :, 0:width].reshape(both * rows, width)
        shares = tok[at : at + both, :, width:].reshape(both * rows, lanes).astype(f32)
        acts = []
        for e in range(experts):
            gate = dot(held, up[e, 0])
            acts.append((silu(gate) * dot(held, up[e, 1])).astype(bf16))
        share = [
            jnp.sum(jnp.where(named == first + e, shares, 0.0), axis=1, keepdims=True)
            for e in range(experts)
        ]
        for n in range(0, width, tile):
            total = share[0] * dot(acts[0], down[0, :, n : n + tile])
            for e in range(1, experts):
                total = total + share[e] * dot(acts[e], down[e, :, n : n + tile])
            mine[group, :, n : n + tile] = total[:half]
            core_send[group, :, n : n + tile] = total[half:]
        core_copies[group] = send(
            core_send.at[group], core_recv.at[group], core_sems, group, to_core
        )

    middle = depth // 2
    for k in range(depth):
        arrived(slot(1, 0, k))
        pass_on(slot(1, 0, k), slot(1, 1, k), to_core)
        if k < middle:
            pass_on(slot(1, 0, k), slot(3, 0, k), to_y)
        arrived(slot(2, 0, k))
        pass_on(slot(2, 0, k), slot(2, 1, k), to_core)
        if k >= middle:
            pass_on(slot(2, 0, k), slot(3, 0, k), to_x)
    for k in range(depth):
        arrived(slot(1, 1, k))
    work(1)
    for k in range(depth):
        arrived(slot(3, 0, k))
        pass_on(slot(3, 0, k), slot(3, 1, k), to_core)
    for k in range(depth):
        arrived(slot(2, 1, k))
    work(2)
    cut = middle * rows
    low, high = slice(0, cut), slice(cut, half)
    core_copies[1].wait()
    send_x[0] = (mine[1, low, :] + core_recv[1, low, :]).astype(bf16)
    plane = [send(send_x.at[0], recv_x.at[0], plane_sems, 0, to_x)]
    core_copies[2].wait()
    send_y[1] = (mine[2, high, :] + core_recv[2, high, :]).astype(bf16)
    plane.append(send(send_y.at[1], recv_y.at[1], plane_sems, 1, to_y))
    for k in range(depth):
        arrived(slot(3, 1, k))
    work(3)
    core_copies[3].wait()
    send_x[2] = (mine[3, low, :] + core_recv[3, low, :]).astype(bf16)
    by_x = send(send_x.at[2], pass_x, plane_sems, 2, to_x)
    send_y[2] = (mine[3, high, :] + core_recv[3, high, :]).astype(bf16)
    by_y = send(send_y.at[2], pass_y, plane_sems, 3, to_y)
    for k in range(depth):
        arrived(slot(0, 1, k))
    work(0)
    core_copies[0].wait()
    own = mine[0] + core_recv[0]
    mine[0] = own
    by_x.wait()
    send_y[0] = (mine[2, low, :] + core_recv[2, low, :] + pass_x[...].astype(f32)).astype(bf16)
    plane.append(send(send_y.at[0], recv_y.at[0], plane_sems, 4, to_y))
    by_y.wait()
    send_x[1] = (mine[1, high, :] + core_recv[1, high, :] + pass_y[...].astype(f32)).astype(bf16)
    plane.append(send(send_x.at[1], recv_x.at[1], plane_sems, 5, to_x))
    for copy in plane:
        copy.wait()
    back_copies = []

    def summed(k):
        part_at, at = k // middle, k % middle * rows
        return (
            mine[0, k * rows : (k + 1) * rows, :]
            + recv_x[part_at, at : at + rows, :].astype(f32)
            + recv_y[part_at, at : at + rows, :].astype(f32)
        )

    for k in range(1, depth):
        back_send[k] = summed(k).astype(bf16)
        back_copies.append(
            send(back_send.at[k], back_recv.at[depth - k], back_sems, depth - k, ahead[k])
        )
    normed = tok[0, :, 0:width]
    score = jax.nn.sigmoid(
        jnp.sum(normed.astype(f32) * gate_ref[...], axis=1, keepdims=True)
    )
    loads[1].wait()
    shared_act = (silu(dot(normed, shared_up[0])) * dot(normed, shared_up[1])).astype(bf16)
    loads[2].wait()
    moe = score * dot(shared_act, shared_down[...]) + summed(0)
    for copy in back_copies:
        copy.wait()
    for k in range(1, depth):
        moe = moe + back_recv[k].astype(f32)
    moe_ref[...] = moe.astype(bf16)
    for copy in copies:
        copy.wait_send()


def moe_call(
    flat_qk, v_proj, z_proj, conv_qk, conv_v, decay_log, beta_gate, doc_ids, head_gain,
    out_weight, residual, post_gain, route_ids, route_weight, expert_gate_up, expert_down,
    shared_gate_up, shared_down, shared_gate,
):
    heads, length = decay_log.shape
    dim = v_proj.shape[1] // heads
    lanes = 128
    rows, width = residual.shape
    depth = length // rows
    half, cut = depth * rows, depth // 2 * rows
    row_block = jax.ShapeDtypeStruct((rows, width), bf16)
    anywhere = pl.BlockSpec(memory_space=pl.ANY)
    dma = pltpu.SemaphoreType.DMA
    return pl.pallas_call(
        moe_kernel,
        out_shape=(row_block, row_block),
        in_specs=[VM] * 14 + [anywhere] * 5,
        out_specs=(VM, VM),
        scratch_shapes=[
            pltpu.VMEM((RIM, flat_qk.shape[1]), bf16),
            pltpu.VMEM((RIM, v_proj.shape[1]), bf16),
            pltpu.VMEM((heads, length, dim), f32),
            pltpu.VMEM((heads, length, dim), bf16),
            pltpu.VMEM((heads, dim, dim), bf16),
            pltpu.VMEM((heads, dim, dim), f32),
            pltpu.VMEM((heads, dim, dim), bf16),
            pltpu.VMEM((heads, dim, dim), bf16),
            pltpu.VMEM((heads, dim, dim), bf16),
            pltpu.VMEM((heads, dim, dim), bf16),
            pltpu.VMEM(out_weight.shape, bf16),
            pltpu.VMEM(expert_gate_up.shape, bf16),
            pltpu.VMEM(expert_down.shape, bf16),
            pltpu.VMEM(shared_gate_up.shape, bf16),
            pltpu.VMEM(shared_down.shape, bf16),
            pltpu.VMEM((length, width), f32),
            pltpu.VMEM((length, width), bf16),
            pltpu.VMEM((depth, rows, width), bf16),
            pltpu.VMEM((8 * depth, rows, width + lanes), bf16),
            pltpu.VMEM((4, half, width), f32),
            pltpu.VMEM((4, half, width), f32),
            pltpu.VMEM((4, half, width), f32),
            pltpu.VMEM((cut, width), bf16),
            pltpu.VMEM((cut, width), bf16),
            pltpu.VMEM((3, cut, width), bf16),
            pltpu.VMEM((3, cut, width), bf16),
            pltpu.VMEM((2, cut, width), bf16),
            pltpu.VMEM((2, cut, width), bf16),
            pltpu.VMEM((depth, rows, width), bf16),
            pltpu.VMEM((depth, rows, width), bf16),
            dma((5,)),
            dma((2, 2)),
            dma((2, heads)),
            dma((2, depth)),
            dma((2, 8 * depth)),
            dma((2, 4)),
            dma((2, 6)),
            dma((2, depth)),
        ],
        compiler_params=params(collective_id=1, has_side_effects=True),
        name="moe",
    )(
        flat_qk, v_proj, conv_qk, conv_v, decay_log, beta_gate, doc_ids.reshape(1, -1), route_ids,
        route_weight, z_proj, head_gain.reshape(1, dim), residual, post_gain.reshape(1, width),
        shared_gate.reshape(1, width), out_weight, expert_gate_up, expert_down, shared_gate_up,
        shared_down,
    )


VM = pl.BlockSpec(memory_space=pltpu.VMEM)


def shards(
    qk_proj, v_proj, z_proj, conv_qk, conv_v, decay_log, beta_gate, doc_ids, head_gain,
    out_weight, residual, post_gain, route_ids, route_weight, expert_gate_up, expert_down,
    shared_gate_up, shared_down, shared_gate,
):
    kernel_len = conv_qk.shape[0]
    length = qk_proj.shape[0]
    key_cols = qk_proj.shape[2]
    heads = decay_log.shape[0]
    dim = v_proj.shape[1] // heads
    width = residual.shape[1]
    seq_count = lax.axis_size("seq")
    place = lax.axis_index("seq")
    me = place * lax.axis_size("exp") + lax.axis_index("exp")
    exp_dev = expert_down.shape[0]

    experts_all = exp_dev * seq_count * lax.axis_size("exp")
    flat_qk = qk_proj.reshape(length, 2 * key_cols)
    if seq_count == 8 and lax.axis_size("exp") == 4 and 2 * experts_all == 128:
        return moe_call(
            flat_qk, v_proj, z_proj, conv_qk, conv_v, decay_log, beta_gate, doc_ids, head_gain,
            out_weight, residual, post_gain, route_ids, route_weight, expert_gate_up, expert_down,
            shared_gate_up, shared_down, shared_gate,
        )

    own_share = jnp.sum(
        jnp.where(
            route_ids[:, :, None] == jnp.arange(experts_all),
            route_weight[:, :, None],
            0.0,
        ),
        axis=1,
    )
    rim = shifted(
        jnp.concatenate([flat_qk[length - RIM :], v_proj[length - RIM :]], axis=1), "seq", 1
    )
    pad = kernel_len - 1
    doc_pad = jnp.concatenate([jnp.full((pad,), -1, jnp.int32), doc_ids])
    window = lax.dynamic_slice_in_dim(doc_pad, place * length, length + pad)
    own_doc = window[pad:]
    cols = [(window[i : i + length] == own_doc).astype(f32) for i in range(pad)]
    cols += [jnp.zeros((length,), f32)] * (4 - pad)
    cols += [own_doc.astype(f32), (own_doc == window[pad - 1]).astype(f32)]
    cols = jnp.stack(cols, axis=1)
    out_local, query, move, add = pl.pallas_call(
        delta_kernel,
        out_shape=(
            jax.ShapeDtypeStruct((heads, length, dim), f32),
            jax.ShapeDtypeStruct((heads, length, dim), bf16),
            jax.ShapeDtypeStruct((heads, dim, dim), bf16),
            jax.ShapeDtypeStruct((heads, dim, dim), f32),
        ),
        in_specs=[VM] * 9,
        out_specs=(VM,) * 4,
        compiler_params=params(),
        name="delta",
    )(
        flat_qk, v_proj, rim, conv_qk.reshape(kernel_len, 2 * key_cols), conv_v, decay_log,
        beta_gate, cols, own_doc.astype(f32).reshape(1, length),
    )
    state = add
    for _ in range(max(1, seq_count // 4) - 1):
        before = shifted(state.astype(bf16), "seq", 1)
        state = add + jnp.einsum("hkl,hlv->hkv", move, before, preferred_element_type=f32)
    start = shifted(state.astype(bf16), "seq", 1)
    shares = lax.all_gather(own_share, ("seq", "exp"), axis=0, tiled=True)
    shares = lax.dynamic_slice_in_dim(shares, me * exp_dev, exp_dev, axis=1)
    part = pl.pallas_call(
        project_kernel,
        out_shape=jax.ShapeDtypeStruct((length, width), f32),
        in_specs=[VM] * 6,
        out_specs=VM,
        compiler_params=params(),
        name="project",
    )(query, out_local, start, z_proj, head_gain.reshape(1, dim), out_weight)
    attn_part = lax.psum_scatter(part, "exp", scatter_dimension=0, tiled=True)
    hidden = residual.astype(f32) + attn_part
    normed = (
        hidden * lax.rsqrt(jnp.mean(hidden * hidden, axis=-1, keepdims=True) + 1e-06) * post_gain
    ).astype(bf16)
    gathered = lax.all_gather(normed, ("seq", "exp"), axis=0, tiled=True)
    tokens = gathered.shape[0]
    tile = 256
    parts = pl.pallas_call(
        expert_kernel,
        out_shape=jax.ShapeDtypeStruct((tokens, width), f32),
        grid=(tokens // tile,),
        in_specs=[
            pl.BlockSpec((tile, width), lambda i: (i, 0)),
            pl.BlockSpec((tile, exp_dev), lambda i: (i, 0)),
            pl.BlockSpec(expert_gate_up.shape, lambda i: (0, 0, 0, 0)),
            pl.BlockSpec(expert_down.shape, lambda i: (0, 0, 0)),
        ],
        out_specs=pl.BlockSpec((tile, width), lambda i: (i, 0)),
        compiler_params=params(),
        name="experts",
    )(gathered, shares, expert_gate_up, expert_down)
    weighted = lax.psum_scatter(parts, ("seq", "exp"), scatter_dimension=0, tiled=True)
    shared_both = jnp.einsum("rd,zdf->zrf", normed, shared_gate_up, preferred_element_type=f32)
    shared_act = (silu(shared_both[0]) * shared_both[1]).astype(bf16)
    shared_branch = jnp.dot(shared_act, shared_down, preferred_element_type=f32)
    shared_scale = jax.nn.sigmoid(jnp.dot(normed.astype(f32), shared_gate, precision=exact))
    moe_sum = weighted + shared_scale[:, None] * shared_branch
    return (hidden.astype(bf16), moe_sum.astype(bf16))


def solution(mesh):
    placed = (
        P("seq", None, "exp"),
        P("seq", "exp"),
        P("seq", "exp"),
        P(None, None, "exp"),
        P(None, "exp"),
        P("exp", "seq"),
        P("exp", "seq"),
        P(),
        P(),
        P("exp", None),
        P(("seq", "exp"), None),
        P(),
        P(("seq", "exp"), None),
        P(("seq", "exp"), None),
        P(("seq", "exp"), None, None, None),
        P(("seq", "exp"), None, None),
        P(),
        P(),
        P(),
    )
    return jax.shard_map(
        shards,
        mesh=mesh,
        in_specs=placed,
        out_specs=(P(("seq", "exp"), None), P(("seq", "exp"), None)),
        check_vma=False,
    )
```

```python
import functools

import jax
import jax.numpy as jnp
from jax import lax
from jax.experimental import pallas as pl
from jax.experimental.pallas import tpu as pltpu
from jax.sharding import PartitionSpec as P

exact = lax.Precision.HIGHEST
f32 = jnp.float32
bf16 = jnp.bfloat16
RIM = 16


def dot(a, b, dims=((1,), (0,))):
    return lax.dot_general(
        a.astype(bf16), b.astype(bf16), (dims, ((), ())), preferred_element_type=f32
    )


def dot_exact(a, b, dims=((1,), (0,))):
    return lax.dot_general(a, b, (dims, ((), ())), precision=exact, preferred_element_type=f32)


def silu(x):
    return x * jax.nn.sigmoid(x)


def shifted(value, axis, by):
    peers = lax.axis_size(axis)
    pairs = [(i, i + by) for i in range(peers) if 0 <= i + by < peers]
    return lax.ppermute(value, axis, pairs)


def dot_split(a, b, dims=((1,), (0,))):
    a_low = a - a.astype(bf16).astype(f32)
    b_low = b - b.astype(bf16).astype(f32)
    return dot(a, b, dims) + (dot(a_low, b, dims) + dot(a, b_low, dims))


def unit_lower_inverses(lowers, row, col):
    size = lowers[0].shape[0]
    inverses = [
        jnp.where(row == col, 1.0, jnp.where(row // 2 == col // 2, -lower, 0.0))
        for lower in lowers
    ]
    span = 2
    while span < size:
        joins = (row // (2 * span) == col // (2 * span)) & (row // span != col // span)
        corners = [
            dot(inverse, jnp.where(joins, lower, 0.0))
            for inverse, lower in zip(inverses, lowers)
        ]
        inverses = [
            inverse - dot(corner, inverse) for inverse, corner in zip(inverses, corners)
        ]
        span *= 2
    return inverses


def conv_silu(prev, own, taps, masks):
    length = own.shape[0]
    ext = jnp.concatenate([prev, own], axis=0).astype(f32)
    total = taps[-1] * ext[RIM:]
    for i in range(len(taps) - 1):
        at = RIM - (len(taps) - 1) + i
        total = total + taps[i] * (ext[at : at + length] * masks[i])
    return silu(total)


def delta_body(
    conv_key, conv_value, decay, beta, doc_col, doc_row, enters, out_ref, query_ref, move_ref,
    add_ref, after,
):
    length = doc_row.shape[1]
    heads, _, dim = add_ref.shape
    row = lax.broadcasted_iota(jnp.int32, (length, length), 0)
    col = lax.broadcasted_iota(jnp.int32, (length, length), 1)
    keep = (row >= col) & (doc_col == doc_row)
    keep_f = keep.astype(f32)
    strict = jnp.where(row > col, keep_f, 0.0)
    eye = (row == col).astype(f32)
    cum_row = dot_exact(decay, (row <= col).astype(f32))
    cum_col = dot_exact((row >= col).astype(f32), decay, ((1,), (1,)))
    beta_col = dot_exact(eye, beta, ((1,), (1,)))
    ends = (doc_col == doc_col[length - 1 : length]).astype(f32)
    batch = 4 if heads % 4 == 0 else 2
    for first in range(0, heads, batch):
        group = range(first, first + batch)
        q, k, qk, kk = {}, {}, {}, {}
        for j in range(first // 2, (first + batch) // 2):
            qj, kj = conv_key(0, j), conv_key(1, j)
            q[j] = qj * (lax.rsqrt(jnp.sum(qj * qj, axis=1, keepdims=True) + 1e-06) * dim ** (-0.5))
            k[j] = kj * lax.rsqrt(jnp.sum(kj * kj, axis=1, keepdims=True) + 1e-06)
            both = dot_exact(jnp.concatenate([q[j], k[j]], axis=0), k[j], ((1,), (1,)))
            qk[j], kk[j] = both[:length], both[length:]
        within, carried, lowers = [], [], []
        for h in group:
            spread = cum_col[:, h : h + 1] - cum_row[h : h + 1, :]
            within.append(jnp.exp(jnp.where(keep, spread, 0.0)) * keep_f)
            carried.append(jnp.exp(cum_col[:, h : h + 1]) * enters)
            lowers.append(beta_col[:, h : h + 1] * within[-1] * kk[h // 2] * strict)
        inverses = unit_lower_inverses(lowers, row, col)
        solved = []
        for n, h in enumerate(group):
            b = beta_col[:, h : h + 1]
            sides = jnp.concatenate([b * conv_value(h), (b * carried[n]) * k[h // 2]], axis=1)
            solved.append(dot_split(inverses[n], sides))
        for n, h in enumerate(group):
            last = cum_col[length - 1 : length, h : h + 1]
            to_end = jnp.exp((last - cum_col[:, h : h + 1]) * ends) * ends
            end = dot(to_end * k[h // 2], solved[n], ((0,), (0,)))
            add_ref[h] = end[:, :dim]
            move_ref[h] = (carried[n][length - 1 : length] * eye - end[:, dim:]).astype(bf16)
        after(first, batch)
        for n, h in enumerate(group):
            local = dot_split(qk[h // 2] * within[n], solved[n])
            out_ref[h] = local[:, :dim]
            query_ref[h] = (carried[n] * q[h // 2] - local[:, dim:]).astype(bf16)


def delta_kernel(
    qk_ref, v_ref, rim_ref, taps_qk_ref, taps_v_ref, decay_ref, beta_ref, cols_ref, row_ref,
    out_ref, query_ref, move_ref, add_ref,
):
    dim = add_ref.shape[1]
    key_cols = taps_qk_ref.shape[1] // 2
    kernel_len = taps_v_ref.shape[0]
    cols = cols_ref[...]
    masks = [cols[:, i : i + 1] for i in range(kernel_len - 1)]

    def head(ref, rim_at, taps_ref, at):
        taps = [taps_ref[i : i + 1, at : at + dim] for i in range(kernel_len)]
        rim = rim_ref[:, rim_at + at : rim_at + at + dim]
        return conv_silu(rim, ref[:, at : at + dim], taps, masks)

    delta_body(
        lambda half, j: head(qk_ref, 0, taps_qk_ref, half * key_cols + j * dim),
        lambda h: head(v_ref, 2 * key_cols, taps_v_ref, h * dim),
        decay_ref[...], beta_ref[...], cols[:, 4:5], row_ref[0:1, :], cols[:, 5:6],
        out_ref, query_ref, move_ref, add_ref, lambda first, batch: None,
    )


def project_kernel(query_ref, out_ref, state_ref, z_ref, gain_ref, weight_ref, part_ref):
    heads, length, dim = out_ref.shape
    gated = []
    for h in range(heads):
        attn = out_ref[h] + dot(query_ref[h], state_ref[h])
        scale = lax.rsqrt(jnp.mean(attn * attn, axis=1, keepdims=True) + 1e-06)
        z = z_ref[:, h * dim : (h + 1) * dim].astype(f32)
        gated.append((attn * scale * gain_ref[...] * silu(z)).astype(bf16))
    part_ref[...] = dot(jnp.concatenate(gated, axis=1), weight_ref[...])


def expert_kernel(rows_ref, share_ref, up_ref, down_ref, out_ref):
    total = None
    for e in range(up_ref.shape[0]):
        gate = dot(rows_ref[...], up_ref[e, 0])
        up = dot(rows_ref[...], up_ref[e, 1])
        act = (silu(gate) * up).astype(bf16)
        term = share_ref[:, e : e + 1] * dot(act, down_ref[e])
        total = term if total is None else total + term
    out_ref[...] = total


def params(**more):
    return pltpu.CompilerParams(vmem_limit_bytes=56 * 1024 * 1024, **more)


MESH = pl.DeviceIdType.MESH


def moe_kernel(
    qk_ref, v_ref, taps_qk_ref, taps_v_ref, decay_ref, beta_ref, doc_ref, ids_ref, route_ref,
    z_ref, head_gain_ref, residual_ref, post_gain_ref, gate_ref, weight_hbm, up_hbm, down_hbm, shared_up_hbm, shared_down_hbm,
    hidden_ref, moe_ref,
    rim_qk, rim_v, local_ref, query_ref, move, add, add_send, add_recv, state_send, state_recv,
    weight, up, down, shared_up, shared_down, part, part_send, part_recv, tok, mine, core_send,
    core_recv, pass_x, pass_y, send_x, send_y, recv_x, recv_y, back_send, back_recv,
    load_sem, rim_sems, hop_sems, part_sems, tok_sems, core_sems, plane_sems, back_sems,
):
    heads, length, dim = local_ref.shape
    rows, width = residual_ref.shape
    depth = length // rows
    experts = up.shape[0]
    lanes = tok.shape[2] - width
    seq = lax.axis_index("seq")
    z = lax.axis_index("exp")
    core = lax.rem(seq, 2)
    x = lax.rem(seq // 2, 2)
    y = seq // 4
    seqs = lax.axis_size("seq")
    to_next = (lax.rem(seq + 1, seqs), z)
    to_last = (lax.rem(seq + seqs - 1, seqs), z)
    to_core = (seq + 1 - 2 * core, z)
    to_x = (seq + 2 - 4 * x, z)
    to_y = (seq + 4 - 8 * y, z)
    ahead = [(seq, lax.rem(z + k, depth)) for k in range(depth)]

    loads = []
    for n, (src, dst) in enumerate(
        ((weight_hbm, weight), (shared_up_hbm, shared_up), (shared_down_hbm, shared_down),
         (up_hbm, up), (down_hbm, down))
    ):
        load = pltpu.make_async_copy(src, dst, load_sem.at[n])
        load.start()
        loads.append(load)

    barrier = pltpu.get_barrier_semaphore()
    peers = [to_next, to_last, to_core, to_x, to_y] + ahead[1:]
    for peer in peers:
        pl.semaphore_signal(barrier, inc=1, device_id=peer, device_id_type=MESH)
    pl.semaphore_wait(barrier, len(peers))

    def send(src, dst, sems, at, peer):
        copy = pltpu.make_async_remote_copy(
            src_ref=src, dst_ref=dst, send_sem=sems.at[0, at], recv_sem=sems.at[1, at],
            device_id=peer, device_id_type=MESH,
        )
        copy.start()
        return copy

    tail = pl.ds(length - RIM, RIM)
    rims = [
        send(qk_ref.at[tail], rim_qk, rim_sems, 0, to_next),
        send(v_ref.at[tail], rim_v, rim_sems, 1, to_next),
    ]
    kernel_len = taps_v_ref.shape[0]
    doc_row = doc_ref[:, pl.ds(pl.multiple_of(seq * length, length), length)].astype(f32)
    before = jnp.maximum(seq - 1, 0)
    doc_before = doc_ref[:, pl.ds(pl.multiple_of(before * length, length), length)].astype(f32)
    doc_before = jnp.where(seq == 0, -1.0, doc_before)
    doc_both = jnp.broadcast_to(
        jnp.concatenate([doc_before, doc_row], axis=1), (8, 2 * length)
    )
    token = lax.broadcasted_iota(jnp.int32, (length, 2 * length), 0) + length
    other = lax.broadcasted_iota(jnp.int32, (length, 2 * length), 1)
    doc_cols = [
        dot_exact((other == token - i).astype(f32), doc_both, ((1,), (1,)))[:, 0:1]
        for i in range(kernel_len)
    ]
    enters = (doc_cols[0] == doc_before[:, length - 1 : length]).astype(f32)
    same = [(doc_cols[i] == doc_cols[0]).astype(f32) for i in range(kernel_len - 1, 0, -1)]

    def key_head(part_at, j):
        at = slice(j * dim, (j + 1) * dim)
        taps = [taps_qk_ref[i, part_at : part_at + 1, at] for i in range(kernel_len)]
        at = slice((part_at * heads // 2 + j) * dim, (part_at * heads // 2 + j + 1) * dim)
        return conv_silu(rim_qk[:, at], qk_ref[:, at], taps, same)

    def value_head(h):
        at = slice(h * dim, (h + 1) * dim)
        taps = [taps_v_ref[i : i + 1, at] for i in range(kernel_len)]
        return conv_silu(rim_v[:, at], v_ref[:, at], taps, same)

    hops = []

    def hop(first, batch):
        group = pl.ds(first, batch)
        add_send[group] = add[group].astype(bf16)
        at = first // batch
        copy = send(add_send.at[group], add_recv.at[group], hop_sems, at, to_next)
        hops.append((first, batch, at, copy))

    for copy in rims:
        copy.wait()
    delta_body(
        key_head, value_head, decay_ref[...], beta_ref[...], doc_cols[0], doc_row, enters,
        local_ref, query_ref, move, add, hop,
    )
    states = []
    for first, batch, at, copy in hops:
        copy.wait()
        for h in range(first, first + batch):
            state_send[h] = (add[h] + dot(move[h], add_recv[h])).astype(bf16)
        group = pl.ds(first, batch)
        states.append(
            send(
                state_send.at[group], state_recv.at[group], hop_sems, len(hops) + at, to_next
            )
        )
    gated = []
    for h in range(heads):
        if h % hops[0][1] == 0:
            states[h // hops[0][1]].wait()
        attn = local_ref[h] + dot(query_ref[h], state_recv[h])
        scale = lax.rsqrt(jnp.mean(attn * attn, axis=1, keepdims=True) + 1e-06)
        gate_z = z_ref[:, h * dim : (h + 1) * dim].astype(f32)
        gated.append((attn * scale * head_gain_ref[...] * silu(gate_z)).astype(bf16))
    gated = jnp.concatenate(gated, axis=1)
    loads[0].wait()
    tile = width // 4
    for n in range(0, width, tile):
        product = dot(gated, weight[:, n : n + tile])
        part[:, n : n + tile] = product
        part_send[:, n : n + tile] = product.astype(bf16)

    def block_rows(k):
        return pl.ds(pl.multiple_of(lax.rem(z + k, depth) * rows, rows), rows)

    part_copies = {}
    for k in range(depth - 1, 0, -1):
        back = depth - k
        part_copies[k] = send(
            part_send.at[block_rows(k)], part_recv.at[back], part_sems, back, ahead[k]
        )
    hidden = residual_ref[...].astype(f32) + part[block_rows(0), :]
    for k in range(1, depth):
        part_copies[k].wait()
    for k in range(1, depth):
        hidden = hidden + part_recv[k].astype(f32)
    hidden_ref[...] = hidden.astype(bf16)
    normed = (
        hidden * lax.rsqrt(jnp.mean(hidden * hidden, axis=1, keepdims=True) + 1e-06)
        * post_gain_ref[...]
    ).astype(bf16)
    tok[0, :, 0:width] = normed
    lane = lax.broadcasted_iota(jnp.int32, (1, lanes), 1)
    named = lax.rem(lane, lanes // 2)
    expert = lax.rem(lax.broadcasted_iota(jnp.int32, (lanes, rows), 0), lanes // 2)
    by_expert = jnp.zeros((lanes, rows), f32)
    for n in range(ids_ref.shape[0]):
        by_expert = by_expert + jnp.where(
            ids_ref[n : n + 1, :] == expert, route_ref[n : n + 1, :], 0.0
        )
    diagonal = lax.broadcasted_iota(jnp.int32, (lanes, lanes), 0) == lane
    share = dot_exact(by_expert, diagonal.astype(f32), ((0,), (0,)))
    rest = share - share.astype(bf16).astype(f32)
    tok[0, :, width:] = jnp.where(lane < lanes // 2, share, rest).astype(bf16)

    def slot(group, other, k):
        return (group * 2 + other) * depth + k

    copies = []

    def pass_on(at, to, peer):
        copies.append(send(tok.at[at], tok.at[to], tok_sems, to, peer))

    def arrived(at):
        pltpu.make_async_remote_copy(
            src_ref=tok.at[at], dst_ref=tok.at[at], send_sem=tok_sems.at[0, at],
            recv_sem=tok_sems.at[1, at], device_id=to_core, device_id_type=MESH,
        ).wait_recv()

    def spread_own(k):
        pass_on(slot(0, 0, k), slot(1, 0, k), to_x)
        pass_on(slot(0, 0, k), slot(2, 0, k), to_y)
        pass_on(slot(0, 0, k), slot(0, 1, k), to_core)

    for k in range(1, depth):
        pass_on(0, slot(0, 0, depth - k), ahead[k])
    spread_own(0)
    for k in [1, depth - 1] + list(range(2, depth - 1)):
        arrived(slot(0, 0, k))
        spread_own(k)
    loads[3].wait()
    loads[4].wait()

    first = (seq * depth + z) * experts
    half = depth * rows
    core_copies = {}

    def work(group):
        at = slot(group, 0, 0)
        both = 2 * depth
        held = tok[at : at + both, :, 0:width].reshape(both * rows, width)
        shares = tok[at : at + both, :, width:].reshape(both * rows, lanes).astype(f32)
        acts = []
        for e in range(experts):
            gate = dot(held, up[e, 0])
            acts.append((silu(gate) * dot(held, up[e, 1])).astype(bf16))
        share = [
            jnp.sum(jnp.where(named == first + e, shares, 0.0), axis=1, keepdims=True)
            for e in range(experts)
        ]
        for n in range(0, width, tile):
            total = share[0] * dot(acts[0], down[0, :, n : n + tile])
            for e in range(1, experts):
                total = total + share[e] * dot(acts[e], down[e, :, n : n + tile])
            mine[group, :, n : n + tile] = total[:half]
            core_send[group, :, n : n + tile] = total[half:]
        core_copies[group] = send(
            core_send.at[group], core_recv.at[group], core_sems, group, to_core
        )

    middle = depth // 2
    for k in range(depth):
        arrived(slot(1, 0, k))
        pass_on(slot(1, 0, k), slot(1, 1, k), to_core)
        if k < middle:
            pass_on(slot(1, 0, k), slot(3, 0, k), to_y)
        arrived(slot(2, 0, k))
        pass_on(slot(2, 0, k), slot(2, 1, k), to_core)
        if k >= middle:
            pass_on(slot(2, 0, k), slot(3, 0, k), to_x)
    for k in range(depth):
        arrived(slot(1, 1, k))
    work(1)
    for k in range(depth):
        arrived(slot(3, 0, k))
        pass_on(slot(3, 0, k), slot(3, 1, k), to_core)
    for k in range(depth):
        arrived(slot(2, 1, k))
    work(2)
    cut = middle * rows
    low, high = slice(0, cut), slice(cut, half)
    core_copies[1].wait()
    send_x[0] = (mine[1, low, :] + core_recv[1, low, :]).astype(bf16)
    plane = [send(send_x.at[0], recv_x.at[0], plane_sems, 0, to_x)]
    core_copies[2].wait()
    send_y[1] = (mine[2, high, :] + core_recv[2, high, :]).astype(bf16)
    plane.append(send(send_y.at[1], recv_y.at[1], plane_sems, 1, to_y))
    for k in range(depth):
        arrived(slot(3, 1, k))
    work(3)
    core_copies[3].wait()
    order = list(range(1, depth)) + [0]
    across, relays = {}, {}
    for k in order:
        at = pl.ds(k % middle * rows, rows)
        block = slice(k * rows, (k + 1) * rows)
        out, land, peer = (send_x, pass_x, to_x) if k < middle else (send_y, pass_y, to_y)
        out[2, at, :] = (mine[3, block, :] + core_recv[3, block, :]).astype(bf16)
        across[k] = send(out.at[2, at], land.at[at], plane_sems, 2 + k, peer)
    for k in range(depth):
        arrived(slot(0, 1, k))
    work(0)
    core_copies[0].wait()
    own = mine[0] + core_recv[0]
    mine[0] = own
    for k in order:
        at = pl.ds(k % middle * rows, rows)
        block = slice(k * rows, (k + 1) * rows)
        across[k].wait()
        if k < middle:
            passed = mine[2, block, :] + core_recv[2, block, :] + pass_x[at, :].astype(f32)
            send_y[0, at, :] = passed.astype(bf16)
            out, land, peer = send_y.at[0, at], recv_y.at[0, at], to_y
        else:
            passed = mine[1, block, :] + core_recv[1, block, :] + pass_y[at, :].astype(f32)
            send_x[1, at, :] = passed.astype(bf16)
            out, land, peer = send_x.at[1, at], recv_x.at[1, at], to_x
        relays[k] = send(out, land, plane_sems, 2 + depth + k, peer)
    for copy in plane:
        copy.wait()
    back_copies = []

    def summed(k):
        part_at, at = k // middle, k % middle * rows
        return (
            mine[0, k * rows : (k + 1) * rows, :]
            + recv_x[part_at, at : at + rows, :].astype(f32)
            + recv_y[part_at, at : at + rows, :].astype(f32)
        )

    for k in range(1, depth):
        relays[k].wait()
        back_send[k] = summed(k).astype(bf16)
        back_copies.append(
            send(back_send.at[k], back_recv.at[depth - k], back_sems, depth - k, ahead[k])
        )
    relays[0].wait()
    normed = tok[0, :, 0:width]
    score = jax.nn.sigmoid(
        jnp.sum(normed.astype(f32) * gate_ref[...], axis=1, keepdims=True)
    )
    loads[1].wait()
    shared_act = (silu(dot(normed, shared_up[0])) * dot(normed, shared_up[1])).astype(bf16)
    loads[2].wait()
    moe = score * dot(shared_act, shared_down[...]) + summed(0)
    for copy in back_copies:
        copy.wait()
    for k in range(1, depth):
        moe = moe + back_recv[k].astype(f32)
    moe_ref[...] = moe.astype(bf16)
    for copy in copies:
        copy.wait_send()


def moe_call(
    flat_qk, v_proj, z_proj, conv_qk, conv_v, decay_log, beta_gate, doc_ids, head_gain,
    out_weight, residual, post_gain, route_ids, route_weight, expert_gate_up, expert_down,
    shared_gate_up, shared_down, shared_gate,
):
    heads, length = decay_log.shape
    dim = v_proj.shape[1] // heads
    lanes = 128
    rows, width = residual.shape
    depth = length // rows
    half, cut = depth * rows, depth // 2 * rows
    row_block = jax.ShapeDtypeStruct((rows, width), bf16)
    anywhere = pl.BlockSpec(memory_space=pl.ANY)
    dma = pltpu.SemaphoreType.DMA
    return pl.pallas_call(
        moe_kernel,
        out_shape=(row_block, row_block),
        in_specs=[VM] * 14 + [anywhere] * 5,
        out_specs=(VM, VM),
        scratch_shapes=[
            pltpu.VMEM((RIM, flat_qk.shape[1]), bf16),
            pltpu.VMEM((RIM, v_proj.shape[1]), bf16),
            pltpu.VMEM((heads, length, dim), f32),
            pltpu.VMEM((heads, length, dim), bf16),
            pltpu.VMEM((heads, dim, dim), bf16),
            pltpu.VMEM((heads, dim, dim), f32),
            pltpu.VMEM((heads, dim, dim), bf16),
            pltpu.VMEM((heads, dim, dim), bf16),
            pltpu.VMEM((heads, dim, dim), bf16),
            pltpu.VMEM((heads, dim, dim), bf16),
            pltpu.VMEM(out_weight.shape, bf16),
            pltpu.VMEM(expert_gate_up.shape, bf16),
            pltpu.VMEM(expert_down.shape, bf16),
            pltpu.VMEM(shared_gate_up.shape, bf16),
            pltpu.VMEM(shared_down.shape, bf16),
            pltpu.VMEM((length, width), f32),
            pltpu.VMEM((length, width), bf16),
            pltpu.VMEM((depth, rows, width), bf16),
            pltpu.VMEM((8 * depth, rows, width + lanes), bf16),
            pltpu.VMEM((4, half, width), f32),
            pltpu.VMEM((4, half, width), f32),
            pltpu.VMEM((4, half, width), f32),
            pltpu.VMEM((cut, width), bf16),
            pltpu.VMEM((cut, width), bf16),
            pltpu.VMEM((3, cut, width), bf16),
            pltpu.VMEM((3, cut, width), bf16),
            pltpu.VMEM((2, cut, width), bf16),
            pltpu.VMEM((2, cut, width), bf16),
            pltpu.VMEM((depth, rows, width), bf16),
            pltpu.VMEM((depth, rows, width), bf16),
            dma((5,)),
            dma((2, 2)),
            dma((2, heads)),
            dma((2, depth)),
            dma((2, 8 * depth)),
            dma((2, 4)),
            dma((2, 2 + 2 * depth)),
            dma((2, depth)),
        ],
        compiler_params=params(collective_id=1, has_side_effects=True),
        name="moe",
    )(
        flat_qk, v_proj, conv_qk, conv_v, decay_log, beta_gate, doc_ids.reshape(1, -1), route_ids.T,
        route_weight.T, z_proj, head_gain.reshape(1, dim), residual, post_gain.reshape(1, width),
        shared_gate.reshape(1, width), out_weight, expert_gate_up, expert_down, shared_gate_up,
        shared_down,
    )


VM = pl.BlockSpec(memory_space=pltpu.VMEM)


def shards(
    qk_proj, v_proj, z_proj, conv_qk, conv_v, decay_log, beta_gate, doc_ids, head_gain,
    out_weight, residual, post_gain, route_ids, route_weight, expert_gate_up, expert_down,
    shared_gate_up, shared_down, shared_gate,
):
    kernel_len = conv_qk.shape[0]
    length = qk_proj.shape[0]
    key_cols = qk_proj.shape[2]
    heads = decay_log.shape[0]
    dim = v_proj.shape[1] // heads
    width = residual.shape[1]
    seq_count = lax.axis_size("seq")
    place = lax.axis_index("seq")
    me = place * lax.axis_size("exp") + lax.axis_index("exp")
    exp_dev = expert_down.shape[0]

    experts_all = exp_dev * seq_count * lax.axis_size("exp")
    flat_qk = qk_proj.reshape(length, 2 * key_cols)
    if seq_count == 8 and lax.axis_size("exp") == 4 and 2 * experts_all == 128:
        return moe_call(
            flat_qk, v_proj, z_proj, conv_qk, conv_v, decay_log, beta_gate, doc_ids, head_gain,
            out_weight, residual, post_gain, route_ids, route_weight, expert_gate_up, expert_down,
            shared_gate_up, shared_down, shared_gate,
        )

    own_share = jnp.sum(
        jnp.where(
            route_ids[:, :, None] == jnp.arange(experts_all),
            route_weight[:, :, None],
            0.0,
        ),
        axis=1,
    )
    rim = shifted(
        jnp.concatenate([flat_qk[length - RIM :], v_proj[length - RIM :]], axis=1), "seq", 1
    )
    pad = kernel_len - 1
    doc_pad = jnp.concatenate([jnp.full((pad,), -1, jnp.int32), doc_ids])
    window = lax.dynamic_slice_in_dim(doc_pad, place * length, length + pad)
    own_doc = window[pad:]
    cols = [(window[i : i + length] == own_doc).astype(f32) for i in range(pad)]
    cols += [jnp.zeros((length,), f32)] * (4 - pad)
    cols += [own_doc.astype(f32), (own_doc == window[pad - 1]).astype(f32)]
    cols = jnp.stack(cols, axis=1)
    out_local, query, move, add = pl.pallas_call(
        delta_kernel,
        out_shape=(
            jax.ShapeDtypeStruct((heads, length, dim), f32),
            jax.ShapeDtypeStruct((heads, length, dim), bf16),
            jax.ShapeDtypeStruct((heads, dim, dim), bf16),
            jax.ShapeDtypeStruct((heads, dim, dim), f32),
        ),
        in_specs=[VM] * 9,
        out_specs=(VM,) * 4,
        compiler_params=params(),
        name="delta",
    )(
        flat_qk, v_proj, rim, conv_qk.reshape(kernel_len, 2 * key_cols), conv_v, decay_log,
        beta_gate, cols, own_doc.astype(f32).reshape(1, length),
    )
    state = add
    for _ in range(max(1, seq_count // 4) - 1):
        before = shifted(state.astype(bf16), "seq", 1)
        state = add + jnp.einsum("hkl,hlv->hkv", move, before, preferred_element_type=f32)
    start = shifted(state.astype(bf16), "seq", 1)
    shares = lax.all_gather(own_share, ("seq", "exp"), axis=0, tiled=True)
    shares = lax.dynamic_slice_in_dim(shares, me * exp_dev, exp_dev, axis=1)
    part = pl.pallas_call(
        project_kernel,
        out_shape=jax.ShapeDtypeStruct((length, width), f32),
        in_specs=[VM] * 6,
        out_specs=VM,
        compiler_params=params(),
        name="project",
    )(query, out_local, start, z_proj, head_gain.reshape(1, dim), out_weight)
    attn_part = lax.psum_scatter(part, "exp", scatter_dimension=0, tiled=True)
    hidden = residual.astype(f32) + attn_part
    normed = (
        hidden * lax.rsqrt(jnp.mean(hidden * hidden, axis=-1, keepdims=True) + 1e-06) * post_gain
    ).astype(bf16)
    gathered = lax.all_gather(normed, ("seq", "exp"), axis=0, tiled=True)
    tokens = gathered.shape[0]
    tile = 256
    parts = pl.pallas_call(
        expert_kernel,
        out_shape=jax.ShapeDtypeStruct((tokens, width), f32),
        grid=(tokens // tile,),
        in_specs=[
            pl.BlockSpec((tile, width), lambda i: (i, 0)),
            pl.BlockSpec((tile, exp_dev), lambda i: (i, 0)),
            pl.BlockSpec(expert_gate_up.shape, lambda i: (0, 0, 0, 0)),
            pl.BlockSpec(expert_down.shape, lambda i: (0, 0, 0)),
        ],
        out_specs=pl.BlockSpec((tile, width), lambda i: (i, 0)),
        compiler_params=params(),
        name="experts",
    )(gathered, shares, expert_gate_up, expert_down)
    weighted = lax.psum_scatter(parts, ("seq", "exp"), scatter_dimension=0, tiled=True)
    shared_both = jnp.einsum("rd,zdf->zrf", normed, shared_gate_up, preferred_element_type=f32)
    shared_act = (silu(shared_both[0]) * shared_both[1]).astype(bf16)
    shared_branch = jnp.dot(shared_act, shared_down, preferred_element_type=f32)
    shared_scale = jax.nn.sigmoid(jnp.dot(normed.astype(f32), shared_gate, precision=exact))
    moe_sum = weighted + shared_scale[:, None] * shared_branch
    return (hidden.astype(bf16), moe_sum.astype(bf16))


def solution(mesh):
    placed = (
        P("seq", None, "exp"),
        P("seq", "exp"),
        P("seq", "exp"),
        P(None, None, "exp"),
        P(None, "exp"),
        P("exp", "seq"),
        P("exp", "seq"),
        P(),
        P(),
        P("exp", None),
        P(("seq", "exp"), None),
        P(),
        P(("seq", "exp"), None),
        P(("seq", "exp"), None),
        P(("seq", "exp"), None, None, None),
        P(("seq", "exp"), None, None),
        P(),
        P(),
        P(),
    )
    return jax.shard_map(
        shards,
        mesh=mesh,
        in_specs=placed,
        out_specs=(P(("seq", "exp"), None), P(("seq", "exp"), None)),
        check_vma=False,
    )
```
